32 devices in a mesh: tower: 8 (over z, x), dev: 4 (over y, core).
Axes of the slice: x: 2, y: 2, z: 4, core: 2. Of those that a mesh axis runs over, the one named last changes fastest.
Arguments:
- ids: int32 [8, 16, 512, 32], P('tower', 'dev'), may hold values from 0 to 511
- tables: bfloat16 [8, 16, 512, 128], P('tower', 'dev'), may hold values from -1 to 1
- order: int32 [512], replicated, may hold values from 0 to 511, each once
- w_first: bfloat16 [8, 2048, 1024], P('tower', 'dev'), may hold values from -0.125 to 0.125
- w_second: bfloat16 [8, 1024, 512], P('tower'), may hold values from -0.1875 to 0.1875
- w_head: bfloat16 [4096, 128], replicated, may hold values from -0.09375 to 0.09375
- w_interact: float32 [64, 128], replicated, may hold values from -0.375 to 0.375
Outputs:
- scores: float32 [4, 128, 128], P('dev', 'tower')
The draws below stay inside these ranges and needn't reach their ends.
Inputs may be any that keep to these rules, and one draw needn't show every extreme that they name: order is a permutation of the batch rows 0 to 511.
All inputs are finite; a program needn't handle non-finite values.
Results may differ from the reference program's by a relative error of at most 0.0023.
Values may be sent and summed in bfloat16 or wider, within the bound.
No kernel may reach another device: no remote copies, remote signals or barrier semaphores. Data moves between devices by JAX's collectives and lax.ppermute only.
A program may use at most 64 MiB of HBM per device.

```python
import math
import jax
import jax.numpy as jnp
from jax import lax

EMB = 128
ACTIVE = 512
BAG = 32
FEATS = 16
HIDDEN_SIZE = 1024
ZWIDTH = 512
HEAD = 128
ROWS_DEV = 128
SAMPLES = 512
TOWERS = 8
N_TOWER = 8
N_DEV = 4


def set_ends(values, stream_key, least, top_value):
    longest = values.shape.index(max(values.shape))
    spots = []
    for shift in (0, 1):
        where = [jax.random.randint(jax.random.fold_in(stream_key, axis), (), 0, length) for axis, length in enumerate(values.shape)]
        where[longest] = (where[longest] + shift) % values.shape[longest]
        spots.append(tuple(where))
    return values.at[spots[0]].set(least).at[spots[1]].set(top_value)


def block_scale(key, shape, shards, low, top_value):
    loudness = 1.0
    for position, blocks in shards:
        heights = jax.random.uniform(jax.random.fold_in(jax.random.fold_in(key, 6), position), (blocks,), jnp.float32, low / len(shards), top_value / len(shards))
        loudness = loudness * jnp.repeat(jnp.exp(heights), shape[position] // blocks).reshape((-1,) + (1,) * (len(shape) - 1 - position))
    return loudness


def gaussian(own_key, extent, deviation, reach, shards=(), kind=jnp.bfloat16):
    result = jax.random.normal(own_key, extent, jnp.float32) * deviation
    if len(shards) > 0:
        result = block_scale(own_key, extent, shards, -0.22, 0.18) * result
    return jnp.clip(result, min=-reach, max=reach).astype(kind)


def setup_inputs(seed: int = 0) -> dict:
    key_list = jax.random.split(jax.random.key(seed), 8)
    ids = set_ends(jax.random.randint(key_list[0], (TOWERS, FEATS, SAMPLES, BAG), 0, ACTIVE), jax.random.fold_in(key_list[0], 1), 0, ACTIVE - 1).astype(jnp.int32)
    tables = gaussian(key_list[1], (TOWERS, FEATS, ACTIVE, EMB), BAG ** -0.5, 1.0, ((0, 8), (1, 4)))
    order = jax.random.permutation(key_list[2], SAMPLES).astype(jnp.int32)
    w_first = gaussian(key_list[3], (TOWERS, FEATS * EMB, HIDDEN_SIZE), (FEATS * EMB) ** -0.5, 0.125, ((0, 8), (1, 4)))
    w_second = gaussian(key_list[4], (TOWERS, HIDDEN_SIZE, ZWIDTH), HIDDEN_SIZE ** -0.5, 0.1875, ((0, 8),))
    w_head = gaussian(key_list[5], (TOWERS * ZWIDTH, HEAD), (TOWERS * ZWIDTH) ** -0.5, 0.09375)
    w_interact = gaussian(key_list[6], (TOWERS * TOWERS, HEAD), (4 * TOWERS * TOWERS) ** -0.5, 0.375, (), jnp.float32)
    return {"ids": ids, "tables": tables, "order": order, "w_first": w_first, "w_second": w_second, "w_head": w_head, "w_interact": w_interact}


def reference(ids, tables, order, w_first, w_second, w_head, w_interact):
    stacked_list = []
    for tower_index in range(N_TOWER):
        pieces = []
        for feature in range(FEATS):
            looked = jnp.take(tables[tower_index, feature], ids[tower_index, feature].astype(jnp.int32), axis=0)
            pooled = lax.optimization_barrier(jnp.sum(looked.astype(jnp.float32), axis=1))
            pieces.append(pooled.astype(jnp.bfloat16))
        features = jnp.take(jnp.concatenate(pieces, axis=1), order.astype(jnp.int32), axis=0)
        preact = jnp.dot(features, w_first[tower_index], preferred_element_type=jnp.float32)
        hidden = jnp.maximum(preact, 0.0).astype(jnp.bfloat16)
        outputs = jnp.dot(hidden, w_second[tower_index], preferred_element_type=jnp.float32).astype(jnp.bfloat16)
        stacked_list.append(outputs)
    stacked = jnp.stack(stacked_list)
    samples = stacked.shape[1]
    joined = jnp.transpose(stacked, (1, 0, 2)).reshape(samples, N_TOWER * ZWIDTH)
    head = jnp.dot(joined, w_head, preferred_element_type=jnp.float32)
    widened = stacked.astype(jnp.float32)
    products = jnp.einsum('tbz,sbz->bts', widened, widened, precision=lax.Precision.HIGHEST) / math.sqrt(ZWIDTH)
    interact_term = jnp.dot(products.reshape(samples, N_TOWER * N_TOWER), w_interact, precision=lax.Precision.HIGHEST)
    return (head + interact_term).reshape(N_DEV, ROWS_DEV, HEAD)
```

```python
import math

import jax
import jax.numpy as jnp
from jax import lax
from jax.experimental import pallas as pl
from jax.experimental.pallas import tpu as pltpu
from jax.sharding import PartitionSpec as P

FIELDS = 8
FIELD_MAX = 15
EVEN_FIELDS = 0x0F0F0F0F


def select_ids(ids, order_row, residues):
    feats, bag, samples = ids.shape
    rows = order_row.shape[1]
    shift = residues.bit_length() - 1
    pick = lax.broadcasted_iota(jnp.int32, (samples, rows), 0) == order_row
    pick = jnp.where(pick, 1.0, 0.0).astype(jnp.bfloat16)
    flat = ids.reshape(feats * bag, samples)
    low = (flat & (residues - 1)).astype(jnp.float32).astype(jnp.bfloat16)
    high = (flat >> shift).astype(jnp.float32).astype(jnp.bfloat16)
    low = jnp.dot(low, pick, preferred_element_type=jnp.float32)
    high = jnp.dot(high, pick, preferred_element_type=jnp.float32)
    return low.astype(jnp.int32), jnp.left_shift(1, 4 * high.astype(jnp.int32))


def pool_feature(residue_ref, weight_ref, base, bag, table):
    residues = table.shape[0] // FIELDS
    spots = lax.broadcasted_iota(jnp.int32, (residues, residue_ref.shape[1]), 0)
    even, odd = None, None
    for first in range(0, bag, FIELD_MAX):
        tally = None
        for at in range(base + first, base + min(first + FIELD_MAX, bag)):
            hit = jnp.where(
                residue_ref[pl.ds(at, 1), :] == spots, weight_ref[pl.ds(at, 1), :], 0
            )
            tally = hit if tally is None else tally + hit
        low, high = tally & EVEN_FIELDS, (tally >> 4) & EVEN_FIELDS
        even, odd = (low, high) if even is None else (even + low, odd + high)
    words = jnp.concatenate([even, odd], axis=0).T
    counts = jnp.concatenate(
        [
            ((words >> (8 * place)) & 255).astype(jnp.float32).astype(jnp.bfloat16)
            for place in range(FIELDS // 2)
        ],
        axis=1,
    )
    return jnp.dot(counts, table, preferred_element_type=jnp.float32).astype(jnp.bfloat16)


def pool_kernel(offsets, ids_ref, tables_ref, order_ref, out_ref, residue_ref, weight_ref):
    feats, bag, samples = ids_ref.shape
    active, emb = tables_ref.shape[1:]
    rows = order_ref.shape[1]
    me = lax.axis_index("dev")
    devices = order_ref.shape[0]
    for block, offset in enumerate(offsets):
        target = lax.rem(me + 2 * offset, devices)
        residue_ref[...], weight_ref[...] = select_ids(
            ids_ref[...], order_ref[pl.ds(target, 1), :], active // FIELDS
        )
        for feature in range(feats):
            out_ref[block * rows : (block + 1) * rows, feature * emb : (feature + 1) * emb] = (
                pool_feature(residue_ref, weight_ref, feature * bag, bag, tables_ref[feature])
            )


def pool(offsets, ids, tables, order):
    feats, bag, samples = ids.shape
    rows = order.shape[1]
    emb = tables.shape[2]
    count = len(offsets) * rows
    return pl.pallas_call(
        lambda *refs: pool_kernel(offsets, *refs),
        out_shape=jax.ShapeDtypeStruct((count, feats * emb), jnp.bfloat16),
        in_specs=[pl.BlockSpec(memory_space=pltpu.VMEM)] * 3,
        out_specs=pl.BlockSpec(memory_space=pltpu.VMEM),
        scratch_shapes=[pltpu.VMEM((feats * bag, rows), jnp.int32)] * 2,
        compiler_params=pltpu.CompilerParams(vmem_limit_bytes=32 * 1024 * 1024),
        cost_estimate=pl.CostEstimate(
            flops=2 * count * feats * emb * tables.shape[1] * 4,
            bytes_accessed=4 * ids.size + 2 * tables.size,
            transcendentals=0,
        ),
    )(ids, tables, order)


def matmul(left, right):
    return jnp.dot(left, right, preferred_element_type=jnp.float32)


def on_device(ids, tables, order, w_first, w_second, w_head, w_interact):
    towers = lax.axis_size("tower")
    devices = lax.axis_size("dev")
    samples = ids.shape[2]
    my_rows = samples // devices
    chips = devices // 2
    order = order.reshape(devices, my_rows)
    ids = jnp.swapaxes(ids[0], 1, 2)
    tables, w_first = tables[0], w_first[0]

    core_swap = [(i, i ^ 1) for i in range(devices)]
    ids_other = lax.ppermute(ids, "dev", core_swap)
    tables_other = lax.ppermute(tables, "dev", core_swap)
    w_other = lax.ppermute(w_first, "dev", core_swap)

    away = tuple(range(1, chips))
    mine = pool(away, ids, tables, order)
    other = pool(away, ids_other, tables_other, order)
    partial = (matmul(mine, w_first) + matmul(other, w_other)).astype(jnp.bfloat16)
    received = []
    for k in away:
        received.append(
            lax.ppermute(
                partial[(k - 1) * my_rows : k * my_rows],
                "dev",
                [(i, (i + 2 * k) % devices) for i in range(devices)],
            )
        )
    mine = pool((0,), ids, tables, order)
    other = pool((0,), ids_other, tables_other, order)
    preact = matmul(mine, w_first) + matmul(other, w_other)
    for part in received:
        preact = preact + part.astype(jnp.float32)

    hidden = jnp.maximum(preact, 0.0).astype(jnp.bfloat16)
    outputs = jnp.dot(hidden, w_second[0], preferred_element_type=jnp.float32).astype(jnp.bfloat16)
    width = outputs.shape[1]
    share = my_rows // towers
    gathered = lax.all_to_all(
        outputs.reshape(1, towers, share, width), "tower", split_axis=1, concat_axis=0, tiled=True
    )[:, 0]
    amount = gathered.shape[1]
    joined = jnp.transpose(gathered, (1, 0, 2)).reshape(amount, towers * width)
    head = jnp.dot(joined, w_head, preferred_element_type=jnp.float32)
    widened = gathered.astype(jnp.float32)
    products = jnp.einsum(
        "tmz,smz->mts", widened, widened, precision=lax.Precision.HIGHEST
    ) / math.sqrt(width)
    interact_term = jnp.dot(
        products.reshape(amount, towers * towers), w_interact, precision=lax.Precision.HIGHEST
    )
    scored = head + interact_term
    return scored[None]


def solution(mesh):
    return jax.shard_map(
        on_device,
        mesh=mesh,
        in_specs=(
            P("tower", "dev", None, None),
            P("tower", "dev", None, None),
            P(),
            P("tower", "dev", None),
            P("tower", None, None),
            P(),
            P(),
        ),
        out_specs=P("dev", "tower", None),
        check_vma=False,
    )
```

```python
import math

import jax
import jax.numpy as jnp
from jax import lax
from jax.experimental import pallas as pl
from jax.experimental.pallas import tpu as pltpu
from jax.sharding import PartitionSpec as P

FIELDS = 8
FIELD_MAX = 15
EVEN_FIELDS = 0x0F0F0F0F


def multiply(left, right):
    return jnp.dot(left, right, preferred_element_type=jnp.float32)


def select_ids(ids, order_row, residues):
    feats, bag, samples = ids.shape
    rows = order_row.shape[1]
    shift = residues.bit_length() - 1
    pick = lax.broadcasted_iota(jnp.int32, (samples, rows), 0) == order_row
    pick = jnp.where(pick, 1.0, 0.0).astype(jnp.bfloat16)
    flat = ids.reshape(feats * bag, samples)
    low = (flat & (residues - 1)).astype(jnp.float32).astype(jnp.bfloat16)
    high = (flat >> shift).astype(jnp.float32).astype(jnp.bfloat16)
    low = jnp.dot(low, pick, preferred_element_type=jnp.float32)
    high = jnp.dot(high, pick, preferred_element_type=jnp.float32)
    return low.astype(jnp.int32), jnp.left_shift(1, 4 * high.astype(jnp.int32))


def pool_feature(residue_ref, weight_ref, base, bag, table):
    residues = table.shape[0] // FIELDS
    spots = lax.broadcasted_iota(jnp.int32, (residues, residue_ref.shape[1]), 0)
    even, odd = None, None
    for first in range(0, bag, FIELD_MAX):
        tally = None
        for at in range(base + first, base + min(first + FIELD_MAX, bag)):
            hit = jnp.where(
                residue_ref[pl.ds(at, 1), :] == spots, weight_ref[pl.ds(at, 1), :], 0
            )
            tally = hit if tally is None else tally + hit
        low, high = tally & EVEN_FIELDS, (tally >> 4) & EVEN_FIELDS
        even, odd = (low, high) if even is None else (even + low, odd + high)
    words = jnp.concatenate([even, odd], axis=0).T
    counts = jnp.concatenate(
        [
            ((words >> (8 * place)) & 255).astype(jnp.float32).astype(jnp.bfloat16)
            for place in range(FIELDS // 2)
        ],
        axis=1,
    )
    return jnp.dot(counts, table, preferred_element_type=jnp.float32).astype(jnp.bfloat16)


def multiply(left, right):
    return jnp.dot(left, right, preferred_element_type=jnp.float32)


def pick_ids(target, ids, order_ref, active, residue_ref, weight_ref):
    residue_ref[...], weight_ref[...] = select_ids(
        ids, order_ref[pl.ds(target, 1), :], active // FIELDS
    )


def fetch(sources, targets, sems):
    copies = [
        pltpu.make_async_copy(source, target, sems.at[place])
        for place, (source, target) in enumerate(zip(sources, targets))
    ]
    for copy in copies:
        copy.start()
    return copies


def block_of(chips_on, core_flip, devices):
    return lax.rem((lax.axis_index("dev") ^ core_flip) + 2 * chips_on, devices)


def first_kernel(
    blocks, order_hbm, ids_hbm, tables_hbm, w_hbm, out_ref, order_ref, ids_ref, tables_ref, w_ref,
    residue_ref, weight_ref, sems,
):
    devices, rows = order_hbm.shape
    feats, bag, samples = ids_hbm.shape
    active, emb = tables_hbm.shape[1:]
    copies = fetch(
        (order_hbm, ids_hbm, tables_hbm, w_hbm), (order_ref, ids_ref, tables_ref, w_ref), sems
    )
    copies[0].wait()
    copies[1].wait()
    for block, chips_on in enumerate(blocks):
        pick_ids(
            block_of(chips_on, 1, devices), ids_ref[...], order_ref, active, residue_ref, weight_ref
        )
        if block == 0:
            copies[2].wait()
        for feature in range(feats):
            out_ref[block * rows : (block + 1) * rows, feature * emb : (feature + 1) * emb] = (
                pool_feature(residue_ref, weight_ref, feature * bag, bag, tables_ref[feature])
            )
    copies[3].wait()


def pool_kernel(
    blocks, order_ref, ids_ref, tables_ref, after_hbm, out_ref, residue_ref, weight_ref
):
    devices, rows = order_ref.shape
    feats, bag, samples = ids_ref.shape
    active, emb = tables_ref.shape[1:]
    for block, chips_on in enumerate(blocks):
        pick_ids(
            block_of(chips_on, 1, devices), ids_ref[...], order_ref, active, residue_ref, weight_ref
        )
        for feature in range(feats):
            out_ref[block * rows : (block + 1) * rows, feature * emb : (feature + 1) * emb] = (
                pool_feature(residue_ref, weight_ref, feature * bag, bag, tables_ref[feature])
            )


def layer_kernel(
    blocks, order_ref, ids_ref, tables_ref, w_ref, *refs
):
    if len(refs) == 3:
        out_ref, residue_ref, weight_ref = refs
        copy = None
    else:
        head_hbm, after_hbm, out_ref, head_ref, residue_ref, weight_ref, sem = refs
        copy = pltpu.make_async_copy(head_hbm, head_ref, sem)
        copy.start()
    devices, rows = order_ref.shape
    feats, bag, samples = ids_ref.shape
    active, emb = tables_ref.shape[1:]
    for block, chips_on in enumerate(blocks):
        pick_ids(
            block_of(chips_on, 0, devices), ids_ref[...], order_ref, active, residue_ref, weight_ref
        )
        total = None
        for first in range(0, feats, 2):
            some = range(first, min(first + 2, feats))
            pooled = [
                pool_feature(residue_ref, weight_ref, feature * bag, bag, tables_ref[feature])
                for feature in some
            ]
            part = multiply(
                jnp.concatenate(pooled, axis=1), w_ref[first * emb : (first + len(some)) * emb, :]
            )
            total = part if total is None else total + part
        out_ref[block * rows : (block + 1) * rows, :] = total
    if copy is not None:
        copy.wait()


IN_HBM = pl.BlockSpec(memory_space=pltpu.HBM)
ON_CHIP = pl.BlockSpec(memory_space=pltpu.VMEM)
VMEM_LIMIT = 32 * 1024 * 1024


def in_hbm(*arrays):
    return [pltpu.with_memory_space_constraint(array, pltpu.HBM) for array in arrays]


def like(array):
    return jax.ShapeDtypeStruct(array.shape, array.dtype)


def picked(ids, rows):
    return [pltpu.VMEM((ids.shape[0] * ids.shape[1], rows), jnp.int32)] * 2


def options():
    return {
        "compiler_params": pltpu.CompilerParams(vmem_limit_bytes=VMEM_LIMIT),
        "cost_estimate": pl.CostEstimate(flops=1, bytes_accessed=1, transcendentals=0),
    }


def first_pool(blocks, order, ids, tables, w):
    rows = order.shape[1]
    count = len(blocks) * rows
    width = ids.shape[0] * tables.shape[2]
    return pl.pallas_call(
        lambda *refs: first_kernel(blocks, *refs),
        out_shape=(
            jax.ShapeDtypeStruct((count, width), jnp.bfloat16),
            like(order), like(ids), like(tables), like(w),
        ),
        in_specs=[IN_HBM] * 4,
        out_specs=(ON_CHIP,) * 5,
        scratch_shapes=picked(ids, rows) + [pltpu.SemaphoreType.DMA((4,))],
        name="first_pool",
        **options(),
    )(*in_hbm(order, ids, tables, w))


def pool(blocks, order, ids, tables, after):
    rows = order.shape[1]
    count = len(blocks) * rows
    width = ids.shape[0] * tables.shape[2]
    return pl.pallas_call(
        lambda *refs: pool_kernel(blocks, *refs),
        out_shape=jax.ShapeDtypeStruct((count, width), jnp.bfloat16),
        in_specs=[ON_CHIP] * 3 + [pl.BlockSpec(memory_space=pl.ANY)],
        out_specs=ON_CHIP,
        scratch_shapes=picked(ids, rows),
        name="pool",
        **options(),
    )(order, ids, tables, after)


def layer(blocks, order, ids, tables, w, head=None, after=None):
    rows = order.shape[1]
    count = len(blocks) * rows
    out_shape = [jax.ShapeDtypeStruct((count, w.shape[1]), jnp.float32)]
    operands = [order, ids, tables, w]
    in_specs = [ON_CHIP] * 4
    scratch = picked(ids, rows)
    if head is not None:
        out_shape.append(like(head))
        operands += in_hbm(head) + [after]
        in_specs += [IN_HBM, pl.BlockSpec(memory_space=pl.ANY)]
        scratch.append(pltpu.SemaphoreType.DMA)
    return pl.pallas_call(
        lambda *refs: layer_kernel(blocks, *refs),
        out_shape=tuple(out_shape),
        in_specs=in_specs,
        out_specs=(ON_CHIP,) * len(out_shape),
        scratch_shapes=scratch,
        name="layer",
        **options(),
    )(*operands)


def join_kernel(partial_ref, pooled_ref, w_ref, out_ref):
    out_ref[...] = partial_ref[...] + multiply(pooled_ref[...], w_ref[...])


def join(partial, pooled, w):
    return pl.pallas_call(
        join_kernel,
        out_shape=like(partial),
        in_specs=[ON_CHIP] * 3,
        out_specs=ON_CHIP,
        compiler_params=pltpu.CompilerParams(vmem_limit_bytes=VMEM_LIMIT),
        cost_estimate=pl.CostEstimate(flops=1, bytes_accessed=1, transcendentals=0),
        name="join",
    )(partial, pooled, w)


def score_kernel(outputs_ref, head_ref, interact_ref, scores_ref):
    towers, rows, width = outputs_ref.shape
    wide = jnp.concatenate([outputs_ref[t] for t in range(towers)], axis=1)
    scores = multiply(wide, head_ref[...])
    interact = interact_ref[...] * (1.0 / math.sqrt(width))
    for t in range(towers):
        mine = outputs_ref[t].astype(jnp.float32)
        for s in range(t, towers):
            gram = jnp.sum(mine * outputs_ref[s].astype(jnp.float32), axis=1, keepdims=True)
            weights = interact[t * towers + s : t * towers + s + 1, :]
            if s != t:
                weights = weights + interact[s * towers + t : s * towers + t + 1, :]
            scores = scores + gram * weights
    scores_ref[...] = scores


def score(outputs, head, interact):
    towers, rows, width = outputs.shape
    return pl.pallas_call(
        score_kernel,
        out_shape=jax.ShapeDtypeStruct((rows, head.shape[1]), jnp.float32),
        in_specs=[ON_CHIP] * 3,
        out_specs=ON_CHIP,
        compiler_params=pltpu.CompilerParams(vmem_limit_bytes=VMEM_LIMIT),
        name="score",
    )(outputs, head, interact)


def on_device(ids, tables, order, w_first, w_second, w_head, w_interact):
    towers = lax.axis_size("tower")
    devices = lax.axis_size("dev")
    samples = ids.shape[2]
    my_rows = samples // devices
    order = order.reshape(devices, my_rows)
    ids, tables, w_first = jnp.swapaxes(ids[0], 1, 2), tables[0], w_first[0]

    def swap_cores(array):
        return lax.ppermute(array, "dev", [(i, i ^ 1) for i in range(devices)])

    w_other = swap_cores(w_first)
    away = tuple(range(1, devices // 2))
    pooled, order, ids, tables, w_first = first_pool(away, order, ids, tables, w_first)
    pooled = swap_cores(pooled)
    (partial,) = layer(away, order, ids, tables, w_first)
    partial = (partial + multiply(pooled, w_other)).astype(jnp.bfloat16)
    received = []
    for k in away:
        received.append(
            lax.ppermute(
                partial[(k - 1) * my_rows : k * my_rows],
                "dev",
                [(i, (i + 2 * k) % devices) for i in range(devices)],
            )
        )
    pooled = swap_cores(pool((0,), order, ids, tables, partial))
    preact, w_head = layer((0,), order, ids, tables, w_first, w_head, partial)
    preact = join(preact, pooled, w_other)
    for part in received:
        preact = preact + part.astype(jnp.float32)

    hidden = jnp.maximum(preact, 0.0).astype(jnp.bfloat16)
    outputs = multiply(hidden, w_second[0]).astype(jnp.bfloat16)
    width = outputs.shape[1]
    share = my_rows // towers
    gathered = lax.all_to_all(
        outputs.reshape(1, towers, share, width), "tower", split_axis=1, concat_axis=0, tiled=True
    )[:, 0]
    return score(gathered, w_head, w_interact)[None]


def solution(mesh):
    return jax.shard_map(
        on_device,
        mesh=mesh,
        in_specs=(
            P("tower", "dev", None, None),
            P("tower", "dev", None, None),
            P(),
            P("tower", "dev", None),
            P("tower", None, None),
            P(),
            P(),
        ),
        out_specs=P("dev", "tower", None),
        check_vma=False,
    )
```

```python
import math

import jax
import jax.numpy as jnp
from jax import lax
from jax.experimental import pallas as pl
from jax.experimental.pallas import tpu as pltpu
from jax.sharding import PartitionSpec as P

WORD_BITS = 32


def multiply(left, right):
    return jnp.dot(left, right, preferred_element_type=jnp.float32)


def one_hot(order_row, samples):
    rows = order_row.shape[1]
    pick = lax.broadcasted_iota(jnp.int32, (samples, rows), 0) == order_row
    return jnp.where(pick, 1.0, 0.0).astype(jnp.bfloat16)


def select_ids(ids, picks, residues):
    feats, bag, samples = ids.shape
    shift = residues.bit_length() - 1
    flat = ids.reshape(feats * bag, samples)
    low = (flat & (residues - 1)).astype(jnp.float32).astype(jnp.bfloat16)
    high = (flat >> shift).astype(jnp.float32).astype(jnp.bfloat16)
    both = multiply(jnp.concatenate([low, high], axis=0), picks).astype(jnp.int32)
    return both[: feats * bag, :], jnp.left_shift(1, both[feats * bag :, :])


def bit_planes(hits):
    waiting = []

    def push(level, bits):
        if level == len(waiting):
            waiting.append([])
        queue = waiting[level]
        queue.append(bits)
        if len(queue) == 3:
            first, second, third = queue
            both = first ^ second
            waiting[level] = [both ^ third]
            push(level + 1, (first & second) | (both & third))

    for bits in hits:
        push(0, bits)
    level = 0
    while level < len(waiting):
        if len(waiting[level]) == 2:
            first, second = waiting[level]
            waiting[level] = [first ^ second]
            push(level + 1, first & second)
        level += 1
    return [queue[0] for queue in waiting]


def merge(low, high, width, mask, second):
    shift = width if second else 0
    low = (low >> shift) & mask if low is not None else None
    if high is None:
        return low
    high = ((high >> shift) & mask) << width
    return high if low is None else low | high


def byte_fields(planes):
    planes = planes + [None] * (8 - len(planes))
    pairs = [
        [merge(planes[p], planes[p + 1], 1, 0x55555555, odd) for odd in (0, 1)]
        for p in range(0, 8, 2)
    ]
    fours = [
        [[merge(pairs[p][a], pairs[p + 1][a], 2, 0x33333333, odd) for odd in (0, 1)] for a in (0, 1)]
        for p in (0, 2)
    ]
    return [
        merge(fours[0][i & 1][(i >> 1) & 1], fours[1][i & 1][(i >> 1) & 1], 4, 0x0F0F0F0F, i >> 2)
        for i in range(8)
    ]


def count_ids(residue_ref, weight_ref, base, bag, active):
    residues = active // WORD_BITS
    spots = lax.broadcasted_iota(jnp.int32, (residues, residue_ref.shape[1]), 0)
    hits = (
        jnp.where(residue_ref[pl.ds(at, 1), :] == spots, weight_ref[pl.ds(at, 1), :], 0)
        for at in range(base, base + bag)
    )
    words = jnp.concatenate(byte_fields(bit_planes(hits)), axis=0).T
    return jnp.concatenate(
        [
            ((words >> (8 * place)) & 255).astype(jnp.float32).astype(jnp.bfloat16)
            for place in range(4)
        ],
        axis=1,
    )


def pool_feature(residue_ref, weight_ref, base, bag, table):
    counts = count_ids(residue_ref, weight_ref, base, bag, table.shape[0])
    return multiply(counts, table).astype(jnp.bfloat16)


def pick_ids(targets, ids, order_ref, active):
    picks = [one_hot(order_ref[pl.ds(target, 1), :], ids.shape[2]) for target in targets]
    return select_ids(ids, jnp.concatenate(picks, axis=1), active // WORD_BITS)


def block_of(chips_on, core_flip, devices):
    return lax.rem((lax.axis_index("dev") ^ core_flip) + 2 * chips_on, devices)


def start_copies(source, target, sem, parts):
    size = source.shape[0] // parts
    for part in range(parts):
        here = pl.ds(part * size, size)
        pltpu.make_async_copy(source.at[here], target.at[here], sem).start()
    return pltpu.make_async_copy(source, target, sem)


def first_kernel(
    blocks, order_hbm, ids_hbm, tables_hbm, w_hbm,
    out_ref, order_ref, ids_ref, tables_ref, w_ref, residues_ref, weights_ref,
    residue_ref, weight_ref, sems,
):
    devices, rows = order_hbm.shape
    feats, bag, samples = ids_hbm.shape
    active, emb = tables_hbm.shape[1:]
    order_here = start_copies(order_hbm, order_ref, sems.at[0], 1)
    ids_here = start_copies(ids_hbm, ids_ref, sems.at[1], feats)
    tables_here = start_copies(tables_hbm, tables_ref, sems.at[2], feats)
    w_here = start_copies(w_hbm, w_ref, sems.at[3], 2 * feats)
    order_here.wait()
    ids_here.wait()
    for block, chips_on in enumerate(blocks):
        residue, weight = pick_ids(
            (block_of(chips_on, 1, devices), block_of(chips_on, 0, devices)),
            ids_ref[...], order_ref, active,
        )
        residue_ref[...], weight_ref[...] = residue[:, :rows], weight[:, :rows]
        residues_ref[block], weights_ref[block] = residue[:, rows:], weight[:, rows:]
        if block == 0:
            tables_here.wait()
        for feature in range(feats):
            out_ref[block * rows : (block + 1) * rows, feature * emb : (feature + 1) * emb] = (
                pool_feature(residue_ref, weight_ref, feature * bag, bag, tables_ref[feature])
            )
    w_here.wait()


def pool_kernel(order_ref, ids_ref, tables_ref, after_hbm, out_ref, residue_ref, weight_ref):
    feats, bag, samples = ids_ref.shape
    active, emb = tables_ref.shape[1:]
    residue_ref[...], weight_ref[...] = pick_ids(
        (block_of(0, 1, order_ref.shape[0]),), ids_ref[...], order_ref, active
    )
    for feature in range(feats):
        out_ref[:, feature * emb : (feature + 1) * emb] = pool_feature(
            residue_ref, weight_ref, feature * bag, bag, tables_ref[feature]
        )


def layer_block(residue_ref, weight_ref, bag, tables_ref, w_ref):
    feats, active, emb = tables_ref.shape
    total = None
    for first in range(0, feats, 2):
        some = range(first, min(first + 2, feats))
        pooled = [
            pool_feature(residue_ref, weight_ref, feature * bag, bag, tables_ref[feature])
            for feature in some
        ]
        part = multiply(
            jnp.concatenate(pooled, axis=1), w_ref[first * emb : (first + len(some)) * emb, :]
        )
        total = part if total is None else total + part
    return total


def away_kernel(residues_ref, weights_ref, tables_ref, w_ref, out_ref):
    count, picked, rows = residues_ref.shape
    bag = picked // tables_ref.shape[0]
    for block in range(count):
        out_ref[block * rows : (block + 1) * rows, :] = layer_block(
            residues_ref.at[block], weights_ref.at[block], bag, tables_ref, w_ref
        )


def home_kernel(
    order_ref, ids_ref, tables_ref, w_ref, after_hbm, out_ref, residue_ref, weight_ref
):
    feats, bag, samples = ids_ref.shape
    residue_ref[...], weight_ref[...] = pick_ids(
        (block_of(0, 0, order_ref.shape[0]),), ids_ref[...], order_ref, tables_ref.shape[1]
    )
    out_ref[...] = layer_block(residue_ref, weight_ref, bag, tables_ref, w_ref)


IN_HBM = pl.BlockSpec(memory_space=pltpu.HBM)
ON_CHIP = pl.BlockSpec(memory_space=pltpu.VMEM)
ANYWHERE = pl.BlockSpec(memory_space=pl.ANY)
VMEM_LIMIT = 16 * 1024 * 1024


def in_hbm(*arrays):
    return [pltpu.with_memory_space_constraint(array, pltpu.HBM) for array in arrays]


def like(array):
    return jax.ShapeDtypeStruct(array.shape, array.dtype)


def picked(ids, rows):
    return [pltpu.VMEM((ids.shape[0] * ids.shape[1], rows), jnp.int32)] * 2


def options():
    return {
        "compiler_params": pltpu.CompilerParams(vmem_limit_bytes=VMEM_LIMIT),
        "cost_estimate": pl.CostEstimate(flops=1, bytes_accessed=1, transcendentals=0),
    }


def first_pool(blocks, order, ids, tables, w):
    rows = order.shape[1]
    feats, bag = ids.shape[:2]
    chosen = jax.ShapeDtypeStruct((len(blocks), feats * bag, rows), jnp.int32)
    return pl.pallas_call(
        lambda *refs: first_kernel(blocks, *refs),
        out_shape=(
            jax.ShapeDtypeStruct((len(blocks) * rows, feats * tables.shape[2]), jnp.bfloat16),
            like(order), like(ids), like(tables), like(w), chosen, chosen,
        ),
        in_specs=[IN_HBM] * 4,
        out_specs=(ON_CHIP,) * 7,
        scratch_shapes=picked(ids, rows) + [pltpu.SemaphoreType.DMA((4,))],
        name="first_pool",
        **options(),
    )(*in_hbm(order, ids, tables, w))


def away_layer(residues, weights, tables, w):
    return pl.pallas_call(
        away_kernel,
        out_shape=jax.ShapeDtypeStruct((residues.shape[0] * residues.shape[2], w.shape[1]), jnp.float32),
        in_specs=[ON_CHIP] * 4,
        out_specs=ON_CHIP,
        name="away_layer",
        **options(),
    )(residues, weights, tables, w)


def home_pool(order, ids, tables, after):
    rows = order.shape[1]
    return pl.pallas_call(
        pool_kernel,
        out_shape=jax.ShapeDtypeStruct((rows, ids.shape[0] * tables.shape[2]), jnp.bfloat16),
        in_specs=[ON_CHIP] * 3 + [ANYWHERE],
        out_specs=ON_CHIP,
        scratch_shapes=picked(ids, rows),
        name="home_pool",
        **options(),
    )(order, ids, tables, after)


def home_layer(order, ids, tables, w, after):
    rows = order.shape[1]
    return pl.pallas_call(
        home_kernel,
        out_shape=jax.ShapeDtypeStruct((rows, w.shape[1]), jnp.float32),
        in_specs=[ON_CHIP] * 4 + [ANYWHERE],
        out_specs=ON_CHIP,
        scratch_shapes=picked(ids, rows),
        name="home_layer",
        **options(),
    )(order, ids, tables, w, after)


def fetch_kernel(head_hbm, interact_hbm, after_hbm, head_ref, interact_ref, sems):
    copies = (
        start_copies(head_hbm, head_ref, sems.at[0], 8),
        start_copies(interact_hbm, interact_ref, sems.at[1], 1),
    )
    for copy in copies:
        copy.wait()


def fetch_head(head, interact, after):
    return pl.pallas_call(
        fetch_kernel,
        out_shape=(like(head), like(interact)),
        in_specs=[IN_HBM] * 2 + [ANYWHERE],
        out_specs=(ON_CHIP,) * 2,
        scratch_shapes=[pltpu.SemaphoreType.DMA((2,))],
        name="fetch_head",
        **options(),
    )(*in_hbm(head, interact), after)


def join_kernel(partial_ref, pooled_ref, w_ref, out_ref):
    out_ref[...] = (partial_ref[...] + multiply(pooled_ref[...], w_ref[...])).astype(out_ref.dtype)


def join(partial, pooled, w, kind):
    return pl.pallas_call(
        join_kernel,
        out_shape=jax.ShapeDtypeStruct(partial.shape, kind),
        in_specs=[ON_CHIP] * 3,
        out_specs=ON_CHIP,
        name="join",
        **options(),
    )(partial, pooled, w)


def second_kernel(w_ref, preact_ref, *refs):
    *received_refs, out_ref = refs
    preact = preact_ref[...]
    for received_ref in received_refs:
        preact = preact + received_ref[...].astype(jnp.float32)
    hidden = jnp.maximum(preact, 0.0).astype(jnp.bfloat16)
    out_ref[...] = multiply(hidden, w_ref[...]).astype(out_ref.dtype)


def second_layer(w, preact, received):
    return pl.pallas_call(
        second_kernel,
        out_shape=jax.ShapeDtypeStruct((preact.shape[0], w.shape[1]), jnp.bfloat16),
        in_specs=[ON_CHIP] * (2 + len(received)),
        out_specs=ON_CHIP,
        name="second_layer",
        **options(),
    )(w, preact, *received)


def score_kernel(outputs_ref, head_ref, interact_ref, scores_ref):
    towers, rows, width = outputs_ref.shape
    me = lax.axis_index("tower")
    outputs = [outputs_ref[me ^ t] for t in range(towers)]
    wide = jnp.concatenate(outputs, axis=1)
    scores = multiply(wide, head_ref[...])
    interact = interact_ref[...] * (1.0 / math.sqrt(width))
    for t in range(towers):
        mine = outputs[t].astype(jnp.float32)
        for s in range(t, towers):
            gram = jnp.sum(mine * outputs[s].astype(jnp.float32), axis=1, keepdims=True)
            weights = interact[t * towers + s : t * towers + s + 1, :]
            if s != t:
                weights = weights + interact[s * towers + t : s * towers + t + 1, :]
            scores = scores + gram * weights
    scores_ref[...] = scores


def score(outputs, head, interact):
    towers, rows, width = outputs.shape
    return pl.pallas_call(
        score_kernel,
        out_shape=jax.ShapeDtypeStruct((rows, head.shape[1]), jnp.float32),
        in_specs=[ON_CHIP] * 3,
        out_specs=ON_CHIP,
        compiler_params=pltpu.CompilerParams(vmem_limit_bytes=VMEM_LIMIT),
        name="score",
    )(outputs, head, interact)


def exchange(blocks):
    towers, rows, width = blocks.shape
    me = lax.axis_index("tower")
    if towers & (towers - 1):
        gathered = lax.all_to_all(blocks, "tower", split_axis=0, concat_axis=0, tiled=True)
        return jnp.take(gathered, me ^ jnp.arange(towers), axis=0)
    held = blocks
    low = 1
    while low < towers:
        group = min(4, towers // low)
        split = held.reshape(held.shape[0] // group, group, *held.shape[1:])
        place = lax.rem(me // low, group)
        parts = [lax.dynamic_index_in_dim(split, place, 1, keepdims=False)]
        for k in range(1, group):
            part = lax.dynamic_index_in_dim(split, place ^ k, 1, keepdims=False)
            parts.append(lax.ppermute(part, "tower", [(i, i ^ (k * low)) for i in range(towers)]))
        held = jnp.stack(parts, axis=1).reshape(split.shape[0], group * held.shape[1], width)
        low *= group
    return held.reshape(towers, rows, width)


def on_device(ids, tables, order, w_first, w_second, w_head, w_interact):
    towers = lax.axis_size("tower")
    devices = lax.axis_size("dev")
    samples = ids.shape[2]
    my_rows = samples // devices
    order = order.reshape(devices, my_rows)
    ids, tables, w_first = jnp.swapaxes(ids[0], 1, 2), tables[0], w_first[0]

    def swap_cores(array):
        return lax.ppermute(array, "dev", [(i, i ^ 1) for i in range(devices)])

    w_other = swap_cores(w_first)
    away = tuple(range(1, devices // 2))
    pooled, order, ids, tables, w_first, residues, weights = first_pool(
        away, order, ids, tables, w_first
    )
    pooled = swap_cores(pooled)
    partial = away_layer(residues, weights, tables, w_first)
    partial = join(partial, pooled, w_other, jnp.bfloat16)
    received = []
    for k in away:
        received.append(
            lax.ppermute(
                partial[(k - 1) * my_rows : k * my_rows],
                "dev",
                [(i, (i + 2 * k) % devices) for i in range(devices)],
            )
        )
    pooled = swap_cores(home_pool(order, ids, tables, partial))
    preact = home_layer(order, ids, tables, w_first, partial)
    preact = join(preact, pooled, w_other, jnp.float32)
    w_head, w_interact = fetch_head(w_head, w_interact, preact)
    outputs = second_layer(w_second[0], preact, received)
    gathered = exchange(outputs.reshape(towers, my_rows // towers, outputs.shape[1]))
    return score(gathered, w_head, w_interact)[None]


def solution(mesh):
    return jax.shard_map(
        on_device,
        mesh=mesh,
        in_specs=(
            P("tower", "dev", None, None),
            P("tower", "dev", None, None),
            P(),
            P("tower", "dev", None),
            P("tower", None, None),
            P(),
            P(),
        ),
        out_specs=P("dev", "tower", None),
        check_vma=False,
    )
```

```python
import math

import jax
import jax.numpy as jnp
from jax import lax
from jax.experimental import pallas as pl
from jax.experimental.pallas import tpu as pltpu
from jax.sharding import PartitionSpec as P

WORD_BITS = 32


def multiply(left, right):
    return jnp.dot(left, right, preferred_element_type=jnp.float32)


def one_hot(order_row, samples):
    rows = order_row.shape[1]
    pick = lax.broadcasted_iota(jnp.int32, (samples, rows), 0) == order_row
    return jnp.where(pick, 1.0, 0.0).astype(jnp.bfloat16)


def select_ids(ids, picks, residues):
    feats, bag, samples = ids.shape
    shift = residues.bit_length() - 1
    flat = ids.reshape(feats * bag, samples)
    low = (flat & (residues - 1)).astype(jnp.float32).astype(jnp.bfloat16)
    high = (flat >> shift).astype(jnp.float32).astype(jnp.bfloat16)
    both = multiply(jnp.concatenate([low, high], axis=0), picks).astype(jnp.int32)
    return both[: feats * bag, :], jnp.left_shift(1, both[feats * bag :, :])


def bit_planes(hits):
    waiting = []

    def push(level, bits):
        if level == len(waiting):
            waiting.append([])
        queue = waiting[level]
        queue.append(bits)
        if len(queue) == 3:
            first, second, third = queue
            both = first ^ second
            waiting[level] = [both ^ third]
            push(level + 1, (first & second) | (both & third))

    for bits in hits:
        push(0, bits)
    level = 0
    while level < len(waiting):
        if len(waiting[level]) == 2:
            first, second = waiting[level]
            waiting[level] = [first ^ second]
            push(level + 1, first & second)
        level += 1
    return [queue[0] for queue in waiting]


def merge(low, high, width, mask, second):
    shift = width if second else 0
    low = (low >> shift) & mask if low is not None else None
    if high is None:
        return low
    high = ((high >> shift) & mask) << width
    return high if low is None else low | high


def byte_fields(planes):
    planes = planes + [None] * (8 - len(planes))
    pairs = [
        [merge(planes[p], planes[p + 1], 1, 0x55555555, odd) for odd in (0, 1)]
        for p in range(0, 8, 2)
    ]
    fours = [
        [[merge(pairs[p][a], pairs[p + 1][a], 2, 0x33333333, odd) for odd in (0, 1)] for a in (0, 1)]
        for p in (0, 2)
    ]
    return [
        merge(fours[0][i & 1][(i >> 1) & 1], fours[1][i & 1][(i >> 1) & 1], 4, 0x0F0F0F0F, i >> 2)
        for i in range(8)
    ]


def count_ids(residue_ref, weight_ref, base, bag, active):
    residues = active // WORD_BITS
    spots = lax.broadcasted_iota(jnp.int32, (residues, residue_ref.shape[1]), 0)
    hits = (
        jnp.where(residue_ref[pl.ds(at, 1), :] == spots, weight_ref[pl.ds(at, 1), :], 0)
        for at in range(base, base + bag)
    )
    words = jnp.concatenate(byte_fields(bit_planes(hits)), axis=0).T
    return jnp.concatenate(
        [
            ((words >> (8 * place)) & 255).astype(jnp.float32).astype(jnp.bfloat16)
            for place in range(4)
        ],
        axis=1,
    )


def pool_feature(residue_ref, weight_ref, base, bag, table):
    counts = count_ids(residue_ref, weight_ref, base, bag, table.shape[0])
    return multiply(counts, table).astype(jnp.bfloat16)


def pick_rows(targets, order_ref, samples):
    picks = [one_hot(order_ref[pl.ds(target, 1), :], samples) for target in targets]
    return jnp.concatenate(picks, axis=1)


def pick_ids(targets, ids, order_ref, active):
    return select_ids(ids, pick_rows(targets, order_ref, ids.shape[2]), active // WORD_BITS)


def block_of(chips_on, core_flip, devices):
    return lax.rem((lax.axis_index("dev") ^ core_flip) + 2 * chips_on, devices)


def start_copies(source, target, sem, parts):
    size = source.shape[0] // parts
    for part in range(parts):
        here = pl.ds(part * size, size)
        pltpu.make_async_copy(source.at[here], target.at[here], sem).start()
    return pltpu.make_async_copy(source, target, sem)


def first_kernel(
    blocks, order_hbm, ids_hbm, tables_hbm, w_hbm,
    out_ref, order_ref, ids_ref, tables_ref, w_ref, residues_ref, weights_ref,
    residue_ref, weight_ref, picks_ref, sems,
):
    devices, rows = order_hbm.shape
    feats, bag, samples = ids_hbm.shape
    active, emb = tables_hbm.shape[1:]
    order_here = start_copies(order_hbm, order_ref, sems.at[0], 1)
    ids_here = start_copies(ids_hbm, ids_ref, sems.at[1], 1)
    tables_here = start_copies(tables_hbm, tables_ref, sems.at[2], 1)
    w_here = start_copies(w_hbm, w_ref, sems.at[3], 2)
    order_here.wait()
    for block, chips_on in enumerate(blocks):
        picks = pick_rows(
            (block_of(chips_on, 1, devices), block_of(chips_on, 0, devices)), order_ref, samples
        )
        if block == 0:
            picks_ref[...] = picks
            ids_here.wait()
            picks = picks_ref[...]
        residue, weight = select_ids(ids_ref[...], picks, active // WORD_BITS)
        residue_ref[...], weight_ref[...] = residue[:, :rows], weight[:, :rows]
        residues_ref[block], weights_ref[block] = residue[:, rows:], weight[:, rows:]
        if block == 0:
            tables_here.wait()
        for feature in range(feats):
            out_ref[block * rows : (block + 1) * rows, feature * emb : (feature + 1) * emb] = (
                pool_feature(residue_ref, weight_ref, feature * bag, bag, tables_ref[feature])
            )
    w_here.wait()


def layer_block(residue_ref, weight_ref, bag, tables_ref, w_ref):
    feats, active, emb = tables_ref.shape
    total = None
    for first in range(0, feats, 2):
        some = range(first, min(first + 2, feats))
        pooled = [
            pool_feature(residue_ref, weight_ref, feature * bag, bag, tables_ref[feature])
            for feature in some
        ]
        part = multiply(
            jnp.concatenate(pooled, axis=1), w_ref[first * emb : (first + len(some)) * emb, :]
        )
        total = part if total is None else total + part
    return total


def away_kernel(residues_ref, weights_ref, tables_ref, w_ref, out_ref):
    count, picked, rows = residues_ref.shape
    bag = picked // tables_ref.shape[0]
    for block in range(count):
        out_ref[block * rows : (block + 1) * rows, :] = layer_block(
            residues_ref.at[block], weights_ref.at[block], bag, tables_ref, w_ref
        )


def home_rows(order_ref, ids_ref, tables_ref, w_ref, pooled_ref, out_ref, residue_ref, weight_ref):
    devices, rows = order_ref.shape
    feats, bag, samples = ids_ref.shape
    active, emb = tables_ref.shape[1:]
    residue, weight = pick_ids(
        (block_of(0, 1, devices), block_of(0, 0, devices)), ids_ref[...], order_ref, active
    )
    residue_ref[...], weight_ref[...] = residue, weight
    other, mine = slice(0, rows), slice(rows, 2 * rows)
    for feature in range(feats):
        pooled_ref[:, feature * emb : (feature + 1) * emb] = pool_feature(
            residue_ref.at[:, other], weight_ref.at[:, other], feature * bag, bag, tables_ref[feature]
        )
    out_ref[...] = layer_block(
        residue_ref.at[:, mine], weight_ref.at[:, mine], bag, tables_ref, w_ref
    )


def early_kernel(
    order_ref, ids_ref, tables_ref, w_ref, partial_ref,
    pooled_ref, out_ref, again_ref, residue_ref, weight_ref,
):
    @pl.when(lax.axis_index("dev") % 2 == 1)
    def _():
        home_rows(
            order_ref, ids_ref, tables_ref, w_ref, pooled_ref, out_ref, residue_ref, weight_ref
        )

    again_ref[...] = partial_ref[...]


def late_kernel(
    order_ref, ids_ref, tables_ref, w_ref, pooled_in_ref, in_ref, after_hbm,
    pooled_ref, out_ref, residue_ref, weight_ref,
):
    second = lax.axis_index("dev") % 2 == 1

    @pl.when(second)
    def _():
        pooled_ref[...] = pooled_in_ref[...]
        out_ref[...] = in_ref[...]

    @pl.when(jnp.logical_not(second))
    def _():
        home_rows(
            order_ref, ids_ref, tables_ref, w_ref, pooled_ref, out_ref, residue_ref, weight_ref
        )


IN_HBM = pl.BlockSpec(memory_space=pltpu.HBM)
ON_CHIP = pl.BlockSpec(memory_space=pltpu.VMEM)
ANYWHERE = pl.BlockSpec(memory_space=pl.ANY)
VMEM_LIMIT = 16 * 1024 * 1024


def in_hbm(*arrays):
    return [pltpu.with_memory_space_constraint(array, pltpu.HBM) for array in arrays]


def like(array):
    return jax.ShapeDtypeStruct(array.shape, array.dtype)


def picked(ids, rows):
    return [pltpu.VMEM((ids.shape[0] * ids.shape[1], rows), jnp.int32)] * 2


def options():
    return {
        "compiler_params": pltpu.CompilerParams(vmem_limit_bytes=VMEM_LIMIT),
        "cost_estimate": pl.CostEstimate(flops=1, bytes_accessed=1, transcendentals=0),
    }


def first_pool(blocks, order, ids, tables, w):
    rows = order.shape[1]
    feats, bag = ids.shape[:2]
    chosen = jax.ShapeDtypeStruct((len(blocks), feats * bag, rows), jnp.int32)
    return pl.pallas_call(
        lambda *refs: first_kernel(blocks, *refs),
        out_shape=(
            jax.ShapeDtypeStruct((len(blocks) * rows, feats * tables.shape[2]), jnp.bfloat16),
            like(order), like(ids), like(tables), like(w), chosen, chosen,
        ),
        in_specs=[IN_HBM] * 4,
        out_specs=(ON_CHIP,) * 7,
        scratch_shapes=picked(ids, rows)
        + [pltpu.VMEM((ids.shape[2], 2 * rows), jnp.bfloat16), pltpu.SemaphoreType.DMA((4,))],
        name="first_pool",
        **options(),
    )(*in_hbm(order, ids, tables, w))


def away_layer(residues, weights, tables, w):
    return pl.pallas_call(
        away_kernel,
        out_shape=jax.ShapeDtypeStruct((residues.shape[0] * residues.shape[2], w.shape[1]), jnp.float32),
        in_specs=[ON_CHIP] * 4,
        out_specs=ON_CHIP,
        name="away_layer",
        **options(),
    )(residues, weights, tables, w)


def home_shapes(order, ids, tables, w):
    rows = order.shape[1]
    return (
        jax.ShapeDtypeStruct((rows, ids.shape[0] * tables.shape[2]), jnp.bfloat16),
        jax.ShapeDtypeStruct((rows, w.shape[1]), jnp.float32),
    )


def home_early(order, ids, tables, w, partial):
    return pl.pallas_call(
        early_kernel,
        out_shape=home_shapes(order, ids, tables, w) + (like(partial),),
        in_specs=[ON_CHIP] * 5,
        out_specs=(ON_CHIP,) * 3,
        scratch_shapes=picked(ids, 2 * order.shape[1]),
        name="home_early",
        **options(),
    )(order, ids, tables, w, partial)


def home_late(order, ids, tables, w, pooled, preact, after):
    return pl.pallas_call(
        late_kernel,
        out_shape=home_shapes(order, ids, tables, w),
        in_specs=[ON_CHIP] * 6 + [ANYWHERE],
        out_specs=(ON_CHIP,) * 2,
        scratch_shapes=picked(ids, 2 * order.shape[1]),
        name="home_late",
        **options(),
    )(order, ids, tables, w, pooled, preact, after)


def fetch_kernel(head_hbm, interact_hbm, after_hbm, head_ref, interact_ref, sems):
    copies = (
        start_copies(head_hbm, head_ref, sems.at[0], 8),
        start_copies(interact_hbm, interact_ref, sems.at[1], 1),
    )
    for copy in copies:
        copy.wait()


def fetch_head(head, interact, after):
    return pl.pallas_call(
        fetch_kernel,
        out_shape=(like(head), like(interact)),
        in_specs=[IN_HBM] * 2 + [ANYWHERE],
        out_specs=(ON_CHIP,) * 2,
        scratch_shapes=[pltpu.SemaphoreType.DMA((2,))],
        name="fetch_head",
        **options(),
    )(*in_hbm(head, interact), after)


def join_kernel(partial_ref, pooled_ref, w_ref, out_ref):
    out_ref[...] = (partial_ref[...] + multiply(pooled_ref[...], w_ref[...])).astype(out_ref.dtype)


def join(partial, pooled, w, kind):
    return pl.pallas_call(
        join_kernel,
        out_shape=jax.ShapeDtypeStruct(partial.shape, kind),
        in_specs=[ON_CHIP] * 3,
        out_specs=ON_CHIP,
        name="join",
        **options(),
    )(partial, pooled, w)


def second_kernel(w_ref, preact_ref, *refs):
    *received_refs, out_ref = refs
    preact = preact_ref[...]
    for received_ref in received_refs:
        preact = preact + received_ref[...].astype(jnp.float32)
    hidden = jnp.maximum(preact, 0.0).astype(jnp.bfloat16)
    out_ref[...] = multiply(hidden, w_ref[...]).astype(out_ref.dtype)


def second_layer(w, preact, received):
    return pl.pallas_call(
        second_kernel,
        out_shape=jax.ShapeDtypeStruct((preact.shape[0], w.shape[1]), jnp.bfloat16),
        in_specs=[ON_CHIP] * (2 + len(received)),
        out_specs=ON_CHIP,
        name="second_layer",
        **options(),
    )(w, preact, *received)


def score_terms(blocks, pairs, head_ref, interact_ref, towers):
    width = head_ref.shape[0] // towers
    total = None
    for block, tower in blocks:
        rows_of_head = pl.ds(pl.multiple_of(tower * width, width), width)
        part = multiply(block, head_ref[rows_of_head, :])
        total = part if total is None else total + part
    for (one, t), (two, s) in pairs:
        gram = jnp.sum(one.astype(jnp.float32) * two.astype(jnp.float32), axis=1, keepdims=True)
        weights = interact_ref[pl.ds(t * towers + s, 1), :]
        if one is not two:
            weights = weights + interact_ref[pl.ds(s * towers + t, 1), :]
        total = total + gram * (weights * (1.0 / math.sqrt(width)))
    return total


def pairs_among(blocks):
    return [(blocks[i], blocks[j]) for i in range(len(blocks)) for j in range(i, len(blocks))]


def blocks_in(ref, masks):
    rows = ref.shape[0] // len(masks)
    me = lax.axis_index("tower")
    return [(ref[i * rows : (i + 1) * rows, :], me ^ mask) for i, mask in enumerate(masks)]


def score_kernel(masks, towers, *refs):
    *held_refs, head_ref, interact_ref, scores_ref = refs
    first = len(masks) == len(held_refs)
    if first:
        blocks = [b for ref, some in zip(held_refs, masks) for b in blocks_in(ref, some)]
        scores_ref[...] = score_terms(
            blocks, pairs_among(blocks), head_ref, interact_ref, towers
        )
    else:
        so_far_ref, *held_refs = held_refs
        kept = blocks_in(held_refs[0], masks[0])
        new = [b for ref, some in zip(held_refs[1:], masks[1:]) for b in blocks_in(ref, some)]
        pairs = [(one, two) for one in kept for two in new] + pairs_among(new)
        scores_ref[...] = so_far_ref[...] + score_terms(
            new, pairs, head_ref, interact_ref, towers
        )


def score(held, masks, head, interact, towers, so_far=None):
    operands = ([] if so_far is None else [so_far]) + list(held) + [head, interact]
    rows = held[0].shape[0] // len(masks[0])
    return pl.pallas_call(
        lambda *refs: score_kernel(masks, towers, *refs),
        out_shape=jax.ShapeDtypeStruct((rows, head.shape[1]), jnp.float32),
        in_specs=[ON_CHIP] * len(operands),
        out_specs=ON_CHIP,
        name="score",
        **options(),
    )(*operands)


def piece_kernel(low, ks, held_ref, after_hbm, *out_refs):
    group = held_ref.shape[1]
    place = lax.rem(lax.axis_index("tower") // low, group)
    for k, out_ref in zip(ks, out_refs):
        out_ref[...] = held_ref[:, place ^ k]


def pieces(held, low, ks, after):
    shape = jax.ShapeDtypeStruct((held.shape[0], *held.shape[2:]), held.dtype)
    return pl.pallas_call(
        lambda *refs: piece_kernel(low, ks, *refs),
        out_shape=(shape,) * len(ks),
        in_specs=[ON_CHIP, ANYWHERE],
        out_specs=(ON_CHIP,) * len(ks),
        name="pieces",
        **options(),
    )(held, after)


def exchange(blocks):
    towers, rows, width = blocks.shape
    assert towers & (towers - 1) == 0
    held, masks = blocks, (0,)
    low = 1
    while True:
        group = min(4, towers // low)
        split = held.reshape(held.shape[0] // group, group, *held.shape[1:])
        parts = [None] * group
        after = split
        for k in range(group - 1, 0, -1):
            if k > 1:
                (after,) = pieces(split, low, (k,), after)
                part = after
            else:
                part, parts[0] = pieces(split, low, (1, 0), after)
            parts[k] = lax.ppermute(part, "tower", [(i, i ^ (k * low)) for i in range(towers)])
        groups = tuple(tuple(k * low + mask for mask in masks) for k in range(group))
        if low * group == towers:
            return [part[0] for part in parts], groups
        joined = jnp.zeros_like(split)
        for k in range(group - 1, -1, -1):
            joined = lax.dynamic_update_index_in_dim(joined, parts[k], k, 1)
        held = joined.reshape(split.shape[0], group * held.shape[1], width)
        masks = sum(groups, ())
        low *= group


def on_device(ids, tables, order, w_first, w_second, w_head, w_interact):
    towers = lax.axis_size("tower")
    devices = lax.axis_size("dev")
    samples = ids.shape[2]
    my_rows = samples // devices
    order = order.reshape(devices, my_rows)
    ids, tables, w_first = jnp.swapaxes(ids[0], 1, 2), tables[0], w_first[0]

    def swap_cores(array):
        return lax.ppermute(array, "dev", [(i, i ^ 1) for i in range(devices)])

    w_other = swap_cores(w_first)
    away = tuple(range(1, devices // 2))
    pooled, order, ids, tables, w_first, residues, weights = first_pool(
        away, order, ids, tables, w_first
    )
    pooled = swap_cores(pooled)
    partial = away_layer(residues, weights, tables, w_first)
    partial = join(partial, pooled, w_other, jnp.bfloat16)
    pooled, preact, partial = home_early(order, ids, tables, w_first, partial)
    received = []
    for k in away:
        received.append(
            lax.ppermute(
                partial[(k - 1) * my_rows : k * my_rows],
                "dev",
                [(i, (i + 2 * k) % devices) for i in range(devices)],
            )
        )
    pooled, preact = home_late(order, ids, tables, w_first, pooled, preact, partial)
    preact = join(preact, swap_cores(pooled), w_other, jnp.float32)
    w_head, w_interact = fetch_head(w_head, w_interact, preact)
    outputs = second_layer(w_second[0], preact, received)
    held, masks = exchange(outputs.reshape(towers, my_rows // towers, outputs.shape[1]))
    so_far = score(held[:1], masks[:1], w_head, w_interact, towers)
    return score(held, masks, w_head, w_interact, towers, so_far)[None]


def solution(mesh):
    return jax.shard_map(
        on_device,
        mesh=mesh,
        in_specs=(
            P("tower", "dev", None, None),
            P("tower", "dev", None, None),
            P(),
            P("tower", "dev", None),
            P("tower", None, None),
            P(),
            P(),
        ),
        out_specs=P("dev", "tower", None),
        check_vma=False,
    )
```

```python
import math

import jax
import jax.numpy as jnp
from jax import lax
from jax.experimental import pallas as pl
from jax.experimental.pallas import tpu as pltpu
from jax.sharding import PartitionSpec as P

WORD_BITS = 32
CODE_TOP = 32767.0


def multiply(left, right):
    return jnp.dot(left, right, preferred_element_type=jnp.float32)


def one_hot(order_row, samples):
    rows = order_row.shape[1]
    pick = lax.broadcasted_iota(jnp.int32, (samples, rows), 0) == order_row
    return jnp.where(pick, 1.0, 0.0).astype(jnp.bfloat16)


def select_ids(ids, picks, residues):
    feats, bag, samples = ids.shape
    shift = residues.bit_length() - 1
    flat = ids.reshape(feats * bag, samples)
    low = (flat & (residues - 1)).astype(jnp.float32).astype(jnp.bfloat16)
    high = (flat >> shift).astype(jnp.float32).astype(jnp.bfloat16)
    both = multiply(jnp.concatenate([low, high], axis=0), picks).astype(jnp.int32)
    return both[: feats * bag, :], jnp.left_shift(1, both[feats * bag :, :])


def bit_planes(hits):
    waiting = []

    def push(level, bits):
        if level == len(waiting):
            waiting.append([])
        queue = waiting[level]
        queue.append(bits)
        if len(queue) == 3:
            first, second, third = queue
            both = first ^ second
            waiting[level] = [both ^ third]
            push(level + 1, (first & second) | (both & third))

    for bits in hits:
        push(0, bits)
    level = 0
    while level < len(waiting):
        if len(waiting[level]) == 2:
            first, second = waiting[level]
            waiting[level] = [first ^ second]
            push(level + 1, first & second)
        level += 1
    return [queue[0] for queue in waiting]


def merge(low, high, width, mask, second):
    shift = width if second else 0
    low = (low >> shift) & mask if low is not None else None
    if high is None:
        return low
    high = ((high >> shift) & mask) << width
    return high if low is None else low | high


def byte_fields(planes):
    planes = planes + [None] * (8 - len(planes))
    pairs = [
        [merge(planes[p], planes[p + 1], 1, 0x55555555, odd) for odd in (0, 1)]
        for p in range(0, 8, 2)
    ]
    fours = [
        [[merge(pairs[p][a], pairs[p + 1][a], 2, 0x33333333, odd) for odd in (0, 1)] for a in (0, 1)]
        for p in (0, 2)
    ]
    return [
        merge(fours[0][i & 1][(i >> 1) & 1], fours[1][i & 1][(i >> 1) & 1], 4, 0x0F0F0F0F, i >> 2)
        for i in range(8)
    ]


def count_ids(residue_ref, weight_ref, base, bag, active):
    residues = active // WORD_BITS
    spots = lax.broadcasted_iota(jnp.int32, (residues, residue_ref.shape[1]), 0)
    hits = (
        jnp.where(residue_ref[pl.ds(at, 1), :] == spots, weight_ref[pl.ds(at, 1), :], 0)
        for at in range(base, base + bag)
    )
    words = jnp.concatenate(byte_fields(bit_planes(hits)), axis=0).T
    return jnp.concatenate(
        [
            ((words >> (8 * place)) & 255).astype(jnp.float32).astype(jnp.bfloat16)
            for place in range(4)
        ],
        axis=1,
    )


def pool_feature(residue_ref, weight_ref, base, bag, table):
    counts = count_ids(residue_ref, weight_ref, base, bag, table.shape[0])
    return multiply(counts, table).astype(jnp.bfloat16)


def pick_rows(targets, order_ref, samples):
    picks = [one_hot(order_ref[pl.ds(target, 1), :], samples) for target in targets]
    return jnp.concatenate(picks, axis=1)


def pick_ids(targets, ids, order_ref, active):
    return select_ids(ids, pick_rows(targets, order_ref, ids.shape[2]), active // WORD_BITS)


def block_of(chips_on, core_flip, devices):
    return lax.rem((lax.axis_index("dev") ^ core_flip) + 2 * chips_on, devices)


def start_copies(source, target, sem, parts):
    size = source.shape[0] // parts
    for part in range(parts):
        here = pl.ds(part * size, size)
        pltpu.make_async_copy(source.at[here], target.at[here], sem).start()
    return pltpu.make_async_copy(source, target, sem)


def first_kernel(
    blocks, order_hbm, ids_hbm, tables_hbm, w_hbm,
    out_ref, order_ref, ids_ref, tables_ref, w_ref, residues_ref, weights_ref,
    residue_ref, weight_ref, picks_ref, sems,
):
    devices, rows = order_hbm.shape
    feats, bag, samples = ids_hbm.shape
    active, emb = tables_hbm.shape[1:]
    order_here = start_copies(order_hbm, order_ref, sems.at[0], 1)
    ids_here = start_copies(ids_hbm, ids_ref, sems.at[1], 1)
    tables_here = start_copies(tables_hbm, tables_ref, sems.at[2], 1)
    w_here = start_copies(w_hbm, w_ref, sems.at[3], 2)
    order_here.wait()
    for block, chips_on in enumerate(blocks):
        picks = pick_rows(
            (block_of(chips_on, 1, devices), block_of(chips_on, 0, devices)), order_ref, samples
        )
        if block == 0:
            picks_ref[...] = picks
            ids_here.wait()
            picks = picks_ref[...]
        residue, weight = select_ids(ids_ref[...], picks, active // WORD_BITS)
        residue_ref[...], weight_ref[...] = residue[:, :rows], weight[:, :rows]
        residues_ref[block], weights_ref[block] = residue[:, rows:], weight[:, rows:]
        if block == 0:
            tables_here.wait()
        for feature in range(feats):
            out_ref[block * rows : (block + 1) * rows, feature * emb : (feature + 1) * emb] = (
                pool_feature(residue_ref, weight_ref, feature * bag, bag, tables_ref[feature])
            )
    w_here.wait()


def layer_block(residue_ref, weight_ref, bag, tables_ref, w_ref):
    feats, active, emb = tables_ref.shape
    total = None
    for first in range(0, feats, 2):
        some = range(first, min(first + 2, feats))
        pooled = [
            pool_feature(residue_ref, weight_ref, feature * bag, bag, tables_ref[feature])
            for feature in some
        ]
        part = multiply(
            jnp.concatenate(pooled, axis=1), w_ref[first * emb : (first + len(some)) * emb, :]
        )
        total = part if total is None else total + part
    return total


def away_kernel(residues_ref, weights_ref, tables_ref, w_ref, out_ref):
    count, picked, rows = residues_ref.shape
    bag = picked // tables_ref.shape[0]
    for block in range(count):
        out_ref[block * rows : (block + 1) * rows, :] = layer_block(
            residues_ref.at[block], weights_ref.at[block], bag, tables_ref, w_ref
        )


def home_rows(order_ref, ids_ref, tables_ref, w_ref, pooled_ref, out_ref, residue_ref, weight_ref):
    devices, rows = order_ref.shape
    feats, bag, samples = ids_ref.shape
    active, emb = tables_ref.shape[1:]
    residue, weight = pick_ids(
        (block_of(0, 1, devices), block_of(0, 0, devices)), ids_ref[...], order_ref, active
    )
    residue_ref[...], weight_ref[...] = residue, weight
    other, mine = slice(0, rows), slice(rows, 2 * rows)
    for feature in range(feats):
        pooled_ref[:, feature * emb : (feature + 1) * emb] = pool_feature(
            residue_ref.at[:, other], weight_ref.at[:, other], feature * bag, bag, tables_ref[feature]
        )
    out_ref[...] = layer_block(
        residue_ref.at[:, mine], weight_ref.at[:, mine], bag, tables_ref, w_ref
    )


def early_kernel(
    order_ref, ids_ref, tables_ref, w_ref, partial_ref, step_ref,
    pooled_ref, out_ref, again_ref, step_again_ref, residue_ref, weight_ref,
):
    @pl.when(lax.axis_index("dev") % 2 == 1)
    def _():
        home_rows(
            order_ref, ids_ref, tables_ref, w_ref, pooled_ref, out_ref, residue_ref, weight_ref
        )

    again_ref[...] = partial_ref[...]
    step_again_ref[...] = step_ref[...]


def late_kernel(
    order_ref, ids_ref, tables_ref, w_ref, pooled_in_ref, in_ref, after_hbm,
    pooled_ref, out_ref, residue_ref, weight_ref,
):
    second = lax.axis_index("dev") % 2 == 1

    @pl.when(second)
    def _():
        pooled_ref[...] = pooled_in_ref[...]
        out_ref[...] = in_ref[...]

    @pl.when(jnp.logical_not(second))
    def _():
        home_rows(
            order_ref, ids_ref, tables_ref, w_ref, pooled_ref, out_ref, residue_ref, weight_ref
        )


IN_HBM = pl.BlockSpec(memory_space=pltpu.HBM)
ON_CHIP = pl.BlockSpec(memory_space=pltpu.VMEM)
ANYWHERE = pl.BlockSpec(memory_space=pl.ANY)
VMEM_LIMIT = 16 * 1024 * 1024


def in_hbm(*arrays):
    return [pltpu.with_memory_space_constraint(array, pltpu.HBM) for array in arrays]


def like(array):
    return jax.ShapeDtypeStruct(array.shape, array.dtype)


def picked(ids, rows):
    return [pltpu.VMEM((ids.shape[0] * ids.shape[1], rows), jnp.int32)] * 2


def options():
    return {
        "compiler_params": pltpu.CompilerParams(vmem_limit_bytes=VMEM_LIMIT),
        "cost_estimate": pl.CostEstimate(flops=1, bytes_accessed=1, transcendentals=0),
    }


def first_pool(blocks, order, ids, tables, w):
    rows = order.shape[1]
    feats, bag = ids.shape[:2]
    chosen = jax.ShapeDtypeStruct((len(blocks), feats * bag, rows), jnp.int32)
    return pl.pallas_call(
        lambda *refs: first_kernel(blocks, *refs),
        out_shape=(
            jax.ShapeDtypeStruct((len(blocks) * rows, feats * tables.shape[2]), jnp.bfloat16),
            like(order), like(ids), like(tables), like(w), chosen, chosen,
        ),
        in_specs=[IN_HBM] * 4,
        out_specs=(ON_CHIP,) * 7,
        scratch_shapes=picked(ids, rows)
        + [pltpu.VMEM((ids.shape[2], 2 * rows), jnp.bfloat16), pltpu.SemaphoreType.DMA((4,))],
        name="first_pool",
        **options(),
    )(*in_hbm(order, ids, tables, w))


def away_layer(residues, weights, tables, w):
    return pl.pallas_call(
        away_kernel,
        out_shape=jax.ShapeDtypeStruct((residues.shape[0] * residues.shape[2], w.shape[1]), jnp.float32),
        in_specs=[ON_CHIP] * 4,
        out_specs=ON_CHIP,
        name="away_layer",
        **options(),
    )(residues, weights, tables, w)


def home_shapes(order, ids, tables, w):
    rows = order.shape[1]
    return (
        jax.ShapeDtypeStruct((rows, ids.shape[0] * tables.shape[2]), jnp.bfloat16),
        jax.ShapeDtypeStruct((rows, w.shape[1]), jnp.float32),
    )


def home_early(order, ids, tables, w, partial, step):
    return pl.pallas_call(
        early_kernel,
        out_shape=home_shapes(order, ids, tables, w) + (like(partial), like(step)),
        in_specs=[ON_CHIP] * 6,
        out_specs=(ON_CHIP,) * 4,
        scratch_shapes=picked(ids, 2 * order.shape[1]),
        name="home_early",
        **options(),
    )(order, ids, tables, w, partial, step)


def home_late(order, ids, tables, w, pooled, preact, after):
    return pl.pallas_call(
        late_kernel,
        out_shape=home_shapes(order, ids, tables, w),
        in_specs=[ON_CHIP] * 6 + [ANYWHERE],
        out_specs=(ON_CHIP,) * 2,
        scratch_shapes=picked(ids, 2 * order.shape[1]),
        name="home_late",
        **options(),
    )(order, ids, tables, w, pooled, preact, after)


def fetch_kernel(head_hbm, interact_hbm, after_hbm, head_ref, interact_ref, sems):
    copies = (
        start_copies(head_hbm, head_ref, sems.at[0], 8),
        start_copies(interact_hbm, interact_ref, sems.at[1], 1),
    )
    for copy in copies:
        copy.wait()


def fetch_head(head, interact, after):
    return pl.pallas_call(
        fetch_kernel,
        out_shape=(like(head), like(interact)),
        in_specs=[IN_HBM] * 2 + [ANYWHERE],
        out_specs=(ON_CHIP,) * 2,
        scratch_shapes=[pltpu.SemaphoreType.DMA((2,))],
        name="fetch_head",
        **options(),
    )(*in_hbm(head, interact), after)


def join_kernel(partial_ref, pooled_ref, w_ref, out_ref):
    out_ref[...] = partial_ref[...] + multiply(pooled_ref[...], w_ref[...])


def join(partial, pooled, w):
    return pl.pallas_call(
        join_kernel,
        out_shape=like(partial),
        in_specs=[ON_CHIP] * 3,
        out_specs=ON_CHIP,
        name="join",
        **options(),
    )(partial, pooled, w)


def join_coded_kernel(partial_ref, pooled_ref, w_ref, coded_ref, step_ref):
    total = partial_ref[...] + multiply(pooled_ref[...], w_ref[...])
    top = jnp.maximum(jnp.max(jnp.abs(total)), 1e-30)
    coded = jnp.round(total * (CODE_TOP / top))
    coded_ref[...] = coded.astype(jnp.int32).astype(coded_ref.dtype)
    step_ref[...] = jnp.full(step_ref.shape, top * (1.0 / CODE_TOP), step_ref.dtype)


def join_coded(partial, pooled, w):
    return pl.pallas_call(
        join_coded_kernel,
        out_shape=(
            jax.ShapeDtypeStruct(partial.shape, jnp.int16),
            jax.ShapeDtypeStruct((8, 128), jnp.float32),
        ),
        in_specs=[ON_CHIP] * 3,
        out_specs=(ON_CHIP,) * 2,
        name="join_coded",
        **options(),
    )(partial, pooled, w)


def second_kernel(w_ref, preact_ref, *refs):
    *received_refs, out_ref = refs
    preact = preact_ref[...]
    for coded_ref, step_ref in zip(received_refs[::2], received_refs[1::2]):
        coded = coded_ref[...].astype(jnp.int32).astype(jnp.float32)
        preact = preact + coded * step_ref[0:1, 0:1]
    hidden = jnp.maximum(preact, 0.0).astype(jnp.bfloat16)
    out_ref[...] = multiply(hidden, w_ref[...]).astype(out_ref.dtype)


def second_layer(w, preact, received):
    return pl.pallas_call(
        second_kernel,
        out_shape=jax.ShapeDtypeStruct((preact.shape[0], w.shape[1]), jnp.bfloat16),
        in_specs=[ON_CHIP] * (2 + len(received)),
        out_specs=ON_CHIP,
        name="second_layer",
        **options(),
    )(w, preact, *received)


def score_terms(blocks, pairs, head_ref, interact_ref, towers):
    width = head_ref.shape[0] // towers
    total = None
    for block, tower in blocks:
        rows_of_head = pl.ds(pl.multiple_of(tower * width, width), width)
        part = multiply(block, head_ref[rows_of_head, :])
        total = part if total is None else total + part
    for (one, t), (two, s) in pairs:
        gram = jnp.sum(one.astype(jnp.float32) * two.astype(jnp.float32), axis=1, keepdims=True)
        weights = interact_ref[pl.ds(t * towers + s, 1), :]
        if one is not two:
            weights = weights + interact_ref[pl.ds(s * towers + t, 1), :]
        total = total + gram * (weights * (1.0 / math.sqrt(width)))
    return total


def pairs_among(blocks):
    return [(blocks[i], blocks[j]) for i in range(len(blocks)) for j in range(i, len(blocks))]


def blocks_in(ref, masks):
    rows = ref.shape[0] // len(masks)
    me = lax.axis_index("tower")
    return [(ref[i * rows : (i + 1) * rows, :], me ^ mask) for i, mask in enumerate(masks)]


def score_kernel(masks, towers, *refs):
    *held_refs, head_ref, interact_ref, scores_ref = refs
    first = len(masks) == len(held_refs)
    if first:
        blocks = [b for ref, some in zip(held_refs, masks) for b in blocks_in(ref, some)]
        scores_ref[...] = score_terms(
            blocks, pairs_among(blocks), head_ref, interact_ref, towers
        )
    else:
        so_far_ref, *held_refs = held_refs
        kept = blocks_in(held_refs[0], masks[0])
        new = [b for ref, some in zip(held_refs[1:], masks[1:]) for b in blocks_in(ref, some)]
        pairs = [(one, two) for one in kept for two in new] + pairs_among(new)
        scores_ref[...] = so_far_ref[...] + score_terms(
            new, pairs, head_ref, interact_ref, towers
        )


def score(held, masks, head, interact, towers, so_far=None):
    operands = ([] if so_far is None else [so_far]) + list(held) + [head, interact]
    rows = held[0].shape[0] // len(masks[0])
    return pl.pallas_call(
        lambda *refs: score_kernel(masks, towers, *refs),
        out_shape=jax.ShapeDtypeStruct((rows, head.shape[1]), jnp.float32),
        in_specs=[ON_CHIP] * len(operands),
        out_specs=ON_CHIP,
        name="score",
        **options(),
    )(*operands)


def piece_kernel(low, ks, held_ref, after_hbm, *out_refs):
    group = held_ref.shape[1]
    place = lax.rem(lax.axis_index("tower") // low, group)
    for k, out_ref in zip(ks, out_refs):
        out_ref[...] = held_ref[:, place ^ k]


def pieces(held, low, ks, after):
    shape = jax.ShapeDtypeStruct((held.shape[0], *held.shape[2:]), held.dtype)
    return pl.pallas_call(
        lambda *refs: piece_kernel(low, ks, *refs),
        out_shape=(shape,) * len(ks),
        in_specs=[ON_CHIP, ANYWHERE],
        out_specs=(ON_CHIP,) * len(ks),
        name="pieces",
        **options(),
    )(held, after)


def exchange(blocks):
    towers, rows, width = blocks.shape
    assert towers & (towers - 1) == 0
    held, masks = blocks, (0,)
    low = 1
    while True:
        group = min(4, towers // low)
        split = held.reshape(held.shape[0] // group, group, *held.shape[1:])
        parts = [None] * group
        after = split
        for k in range(group - 1, 0, -1):
            if k > 1:
                (after,) = pieces(split, low, (k,), after)
                part = after
            else:
                part, parts[0] = pieces(split, low, (1, 0), after)
            parts[k] = lax.ppermute(part, "tower", [(i, i ^ (k * low)) for i in range(towers)])
        groups = tuple(tuple(k * low + mask for mask in masks) for k in range(group))
        if low * group == towers:
            return [part[0] for part in parts], groups
        joined = jnp.zeros_like(split)
        for k in range(group - 1, -1, -1):
            joined = lax.dynamic_update_index_in_dim(joined, parts[k], k, 1)
        held = joined.reshape(split.shape[0], group * held.shape[1], width)
        masks = sum(groups, ())
        low *= group


def on_device(ids, tables, order, w_first, w_second, w_head, w_interact):
    towers = lax.axis_size("tower")
    devices = lax.axis_size("dev")
    samples = ids.shape[2]
    my_rows = samples // devices
    order = order.reshape(devices, my_rows)
    ids, tables, w_first = jnp.swapaxes(ids[0], 1, 2), tables[0], w_first[0]

    def swap_cores(array):
        return lax.ppermute(array, "dev", [(i, i ^ 1) for i in range(devices)])

    w_other = swap_cores(w_first)
    away = tuple(range(1, devices // 2))
    pooled, order, ids, tables, w_first, residues, weights = first_pool(
        away, order, ids, tables, w_first
    )
    pooled = swap_cores(pooled)
    partial = away_layer(residues, weights, tables, w_first)
    partial, step = join_coded(partial, pooled, w_other)
    pooled, preact, partial, step = home_early(order, ids, tables, w_first, partial, step)
    received = []
    for place, chips_on in enumerate(away):
        onward = [(i, (i + 2 * chips_on) % devices) for i in range(devices)]
        block = partial[place * my_rows : (place + 1) * my_rows]
        received += [lax.ppermute(block, "dev", onward), lax.ppermute(step, "dev", onward)]
    pooled, preact = home_late(order, ids, tables, w_first, pooled, preact, partial)
    preact = join(preact, swap_cores(pooled), w_other)
    w_head, w_interact = fetch_head(w_head, w_interact, preact)
    outputs = second_layer(w_second[0], preact, received)
    held, masks = exchange(outputs.reshape(towers, my_rows // towers, outputs.shape[1]))
    so_far = score(held[:1], masks[:1], w_head, w_interact, towers)
    return score(held, masks, w_head, w_interact, towers, so_far)[None]


def solution(mesh):
    return jax.shard_map(
        on_device,
        mesh=mesh,
        in_specs=(
            P("tower", "dev", None, None),
            P("tower", "dev", None, None),
            P(),
            P("tower", "dev", None),
            P("tower", None, None),
            P(),
            P(),
        ),
        out_specs=P("dev", "tower", None),
        check_vma=False,
    )
```

```python
import math

import jax
import jax.numpy as jnp
from jax import lax
from jax.experimental import pallas as pl
from jax.experimental.pallas import tpu as pltpu
from jax.sharding import PartitionSpec as P

WORD_BITS = 32
CODE_TOP = 32767.0


def multiply(left, right):
    return jnp.dot(left, right, preferred_element_type=jnp.float32)


def one_hot(order_row, samples):
    rows = order_row.shape[1]
    pick = lax.broadcasted_iota(jnp.int32, (samples, rows), 0) == order_row
    return jnp.where(pick, 1.0, 0.0).astype(jnp.bfloat16)


def select_ids(ids, picks, residues):
    feats, bag, samples = ids.shape
    shift = residues.bit_length() - 1
    flat = ids.reshape(feats * bag, samples)
    low = (flat & (residues - 1)).astype(jnp.float32).astype(jnp.bfloat16)
    high = (flat >> shift).astype(jnp.float32).astype(jnp.bfloat16)
    both = multiply(jnp.concatenate([low, high], axis=0), picks).astype(jnp.int32)
    return both[: feats * bag, :], jnp.left_shift(1, both[feats * bag :, :])


def bit_planes(hits):
    waiting = []

    def push(level, bits):
        if level == len(waiting):
            waiting.append([])
        queue = waiting[level]
        queue.append(bits)
        if len(queue) == 3:
            first, second, third = queue
            both = first ^ second
            waiting[level] = [both ^ third]
            push(level + 1, (first & second) | (both & third))

    for bits in hits:
        push(0, bits)
    level = 0
    while level < len(waiting):
        if len(waiting[level]) == 2:
            first, second = waiting[level]
            waiting[level] = [first ^ second]
            push(level + 1, first & second)
        level += 1
    return [queue[0] for queue in waiting]


def merge(low, high, width, mask, second):
    shift = width if second else 0
    low = (low >> shift) & mask if low is not None else None
    if high is None:
        return low
    high = ((high >> shift) & mask) << width
    return high if low is None else low | high


def byte_fields(planes):
    planes = planes + [None] * (8 - len(planes))
    pairs = [
        [merge(planes[p], planes[p + 1], 1, 0x55555555, odd) for odd in (0, 1)]
        for p in range(0, 8, 2)
    ]
    fours = [
        [[merge(pairs[p][a], pairs[p + 1][a], 2, 0x33333333, odd) for odd in (0, 1)] for a in (0, 1)]
        for p in (0, 2)
    ]
    return [
        merge(fours[0][i & 1][(i >> 1) & 1], fours[1][i & 1][(i >> 1) & 1], 4, 0x0F0F0F0F, i >> 2)
        for i in range(8)
    ]


def count_ids(residue_ref, weight_ref, base, bag, active):
    residues = active // WORD_BITS
    spots = lax.broadcasted_iota(jnp.int32, (residues, residue_ref.shape[1]), 0)
    hits = (
        jnp.where(residue_ref[pl.ds(at, 1), :] == spots, weight_ref[pl.ds(at, 1), :], 0)
        for at in range(base, base + bag)
    )
    words = jnp.concatenate(byte_fields(bit_planes(hits)), axis=0).T
    return jnp.concatenate(
        [
            ((words >> (8 * place)) & 255).astype(jnp.float32).astype(jnp.bfloat16)
            for place in range(4)
        ],
        axis=1,
    )


def pool_feature(residue_ref, weight_ref, base, bag, table):
    counts = count_ids(residue_ref, weight_ref, base, bag, table.shape[0])
    return multiply(counts, table).astype(jnp.bfloat16)


def pick_rows(targets, order_ref, samples):
    picks = [one_hot(order_ref[pl.ds(target, 1), :], samples) for target in targets]
    return jnp.concatenate(picks, axis=1)


def pick_ids(targets, ids, order_ref, active):
    return select_ids(ids, pick_rows(targets, order_ref, ids.shape[2]), active // WORD_BITS)


def block_of(chips_on, core_flip, devices):
    return lax.rem((lax.axis_index("dev") ^ core_flip) + 2 * chips_on, devices)


def start_copies(source, target, sem, parts):
    size = source.shape[0] // parts
    for part in range(parts):
        here = pl.ds(part * size, size)
        pltpu.make_async_copy(source.at[here], target.at[here], sem).start()
    return pltpu.make_async_copy(source, target, sem)


def first_kernel(
    blocks, order_hbm, ids_hbm, tables_hbm, w_hbm,
    out_ref, order_ref, ids_ref, tables_ref, w_ref, residues_ref, weights_ref,
    residue_ref, weight_ref, picks_ref, sems,
):
    devices, rows = order_hbm.shape
    feats, bag, samples = ids_hbm.shape
    active, emb = tables_hbm.shape[1:]
    order_here = start_copies(order_hbm, order_ref, sems.at[0], 1)
    ids_here = start_copies(ids_hbm, ids_ref, sems.at[1], 1)
    tables_here = start_copies(tables_hbm, tables_ref, sems.at[2], 1)
    w_here = start_copies(w_hbm, w_ref, sems.at[3], 2)
    order_here.wait()
    for block, chips_on in enumerate(blocks):
        picks = pick_rows(
            (block_of(chips_on, 1, devices), block_of(chips_on, 0, devices)), order_ref, samples
        )
        if block == 0:
            picks_ref[...] = picks
            ids_here.wait()
            picks = picks_ref[...]
        residue, weight = select_ids(ids_ref[...], picks, active // WORD_BITS)
        residue_ref[...], weight_ref[...] = residue[:, :rows], weight[:, :rows]
        residues_ref[block], weights_ref[block] = residue[:, rows:], weight[:, rows:]
        if block == 0:
            tables_here.wait()
        for feature in range(feats):
            out_ref[block * rows : (block + 1) * rows, feature * emb : (feature + 1) * emb] = (
                pool_feature(residue_ref, weight_ref, feature * bag, bag, tables_ref[feature])
            )
    w_here.wait()


def layer_block(residue_ref, weight_ref, bag, tables_ref, w_ref):
    feats, active, emb = tables_ref.shape
    total = None
    for first in range(0, feats, 2):
        some = range(first, min(first + 2, feats))
        pooled = [
            pool_feature(residue_ref, weight_ref, feature * bag, bag, tables_ref[feature])
            for feature in some
        ]
        part = multiply(
            jnp.concatenate(pooled, axis=1), w_ref[first * emb : (first + len(some)) * emb, :]
        )
        total = part if total is None else total + part
    return total


def away_kernel(residues_ref, weights_ref, tables_ref, w_ref, out_ref):
    count, picked, rows = residues_ref.shape
    bag = picked // tables_ref.shape[0]
    for block in range(count):
        out_ref[block * rows : (block + 1) * rows, :] = layer_block(
            residues_ref.at[block], weights_ref.at[block], bag, tables_ref, w_ref
        )


def home_rows(order_ref, ids_ref, tables_ref, w_ref, pooled_ref, out_ref, residue_ref, weight_ref):
    devices, rows = order_ref.shape
    feats, bag, samples = ids_ref.shape
    active, emb = tables_ref.shape[1:]
    residue, weight = pick_ids(
        (block_of(0, 1, devices), block_of(0, 0, devices)), ids_ref[...], order_ref, active
    )
    residue_ref[...], weight_ref[...] = residue, weight
    other, mine = slice(0, rows), slice(rows, 2 * rows)
    for feature in range(feats):
        pooled_ref[:, feature * emb : (feature + 1) * emb] = pool_feature(
            residue_ref.at[:, other], weight_ref.at[:, other], feature * bag, bag, tables_ref[feature]
        )
    out_ref[...] = layer_block(
        residue_ref.at[:, mine], weight_ref.at[:, mine], bag, tables_ref, w_ref
    )


def early_kernel(
    order_ref, ids_ref, tables_ref, w_ref, partial_ref, step_ref,
    pooled_ref, out_ref, again_ref, step_again_ref, residue_ref, weight_ref,
):
    @pl.when(lax.axis_index("dev") % 2 == 1)
    def _():
        home_rows(
            order_ref, ids_ref, tables_ref, w_ref, pooled_ref, out_ref, residue_ref, weight_ref
        )

    again_ref[...] = partial_ref[...]
    step_again_ref[...] = step_ref[...]


def late_kernel(
    order_ref, ids_ref, tables_ref, w_ref, pooled_in_ref, in_ref, after_hbm,
    pooled_ref, out_ref, residue_ref, weight_ref,
):
    second = lax.axis_index("dev") % 2 == 1

    @pl.when(second)
    def _():
        pooled_ref[...] = pooled_in_ref[...]
        out_ref[...] = in_ref[...]

    @pl.when(jnp.logical_not(second))
    def _():
        home_rows(
            order_ref, ids_ref, tables_ref, w_ref, pooled_ref, out_ref, residue_ref, weight_ref
        )


IN_HBM = pl.BlockSpec(memory_space=pltpu.HBM)
ON_CHIP = pl.BlockSpec(memory_space=pltpu.VMEM)
ANYWHERE = pl.BlockSpec(memory_space=pl.ANY)
VMEM_LIMIT = 16 * 1024 * 1024


def in_hbm(*arrays):
    return [pltpu.with_memory_space_constraint(array, pltpu.HBM) for array in arrays]


def like(array):
    return jax.ShapeDtypeStruct(array.shape, array.dtype)


def picked(ids, rows):
    return [pltpu.VMEM((ids.shape[0] * ids.shape[1], rows), jnp.int32)] * 2


def options():
    return {
        "compiler_params": pltpu.CompilerParams(vmem_limit_bytes=VMEM_LIMIT),
        "cost_estimate": pl.CostEstimate(flops=1, bytes_accessed=1, transcendentals=0),
    }


def first_pool(blocks, order, ids, tables, w):
    rows = order.shape[1]
    feats, bag = ids.shape[:2]
    chosen = jax.ShapeDtypeStruct((len(blocks), feats * bag, rows), jnp.int32)
    return pl.pallas_call(
        lambda *refs: first_kernel(blocks, *refs),
        out_shape=(
            jax.ShapeDtypeStruct((len(blocks) * rows, feats * tables.shape[2]), jnp.bfloat16),
            like(order), like(ids), like(tables), like(w), chosen, chosen,
        ),
        in_specs=[IN_HBM] * 4,
        out_specs=(ON_CHIP,) * 7,
        scratch_shapes=picked(ids, rows)
        + [pltpu.VMEM((ids.shape[2], 2 * rows), jnp.bfloat16), pltpu.SemaphoreType.DMA((4,))],
        name="first_pool",
        **options(),
    )(*in_hbm(order, ids, tables, w))


def away_layer(residues, weights, tables, w):
    return pl.pallas_call(
        away_kernel,
        out_shape=jax.ShapeDtypeStruct((residues.shape[0] * residues.shape[2], w.shape[1]), jnp.float32),
        in_specs=[ON_CHIP] * 4,
        out_specs=ON_CHIP,
        name="away_layer",
        **options(),
    )(residues, weights, tables, w)


def home_shapes(order, ids, tables, w):
    rows = order.shape[1]
    return (
        jax.ShapeDtypeStruct((rows, ids.shape[0] * tables.shape[2]), jnp.bfloat16),
        jax.ShapeDtypeStruct((rows, w.shape[1]), jnp.float32),
    )


def home_early(order, ids, tables, w, partial, step):
    return pl.pallas_call(
        early_kernel,
        out_shape=home_shapes(order, ids, tables, w) + (like(partial), like(step)),
        in_specs=[ON_CHIP] * 6,
        out_specs=(ON_CHIP,) * 4,
        scratch_shapes=picked(ids, 2 * order.shape[1]),
        name="home_early",
        **options(),
    )(order, ids, tables, w, partial, step)


def home_late(order, ids, tables, w, pooled, preact, after):
    return pl.pallas_call(
        late_kernel,
        out_shape=home_shapes(order, ids, tables, w),
        in_specs=[ON_CHIP] * 6 + [ANYWHERE],
        out_specs=(ON_CHIP,) * 2,
        scratch_shapes=picked(ids, 2 * order.shape[1]),
        name="home_late",
        **options(),
    )(order, ids, tables, w, pooled, preact, after)


def fetch_kernel(head_hbm, interact_hbm, after_hbm, head_ref, interact_ref, sems):
    copies = (
        start_copies(head_hbm, head_ref, sems.at[0], 8),
        start_copies(interact_hbm, interact_ref, sems.at[1], 1),
    )
    for copy in copies:
        copy.wait()


def fetch_head(head, interact, after):
    return pl.pallas_call(
        fetch_kernel,
        out_shape=(like(head), like(interact)),
        in_specs=[IN_HBM] * 2 + [ANYWHERE],
        out_specs=(ON_CHIP,) * 2,
        scratch_shapes=[pltpu.SemaphoreType.DMA((2,))],
        name="fetch_head",
        **options(),
    )(*in_hbm(head, interact), after)


def join_kernel(partial_ref, pooled_ref, w_ref, out_ref):
    out_ref[...] = partial_ref[...] + multiply(pooled_ref[...], w_ref[...])


def join(partial, pooled, w):
    return pl.pallas_call(
        join_kernel,
        out_shape=like(partial),
        in_specs=[ON_CHIP] * 3,
        out_specs=ON_CHIP,
        name="join",
        **options(),
    )(partial, pooled, w)


def code_chunks(width):
    count = max(1, min(8, width // 256))
    return [slice(i * width // count, (i + 1) * width // count) for i in range(count)]


def join_coded_kernel(partial_ref, pooled_ref, w_ref, coded_ref, step_ref):
    step_ref[...] = jnp.zeros_like(step_ref)
    for place, here in enumerate(code_chunks(partial_ref.shape[1])):
        total = partial_ref[:, here] + multiply(pooled_ref[...], w_ref[:, here])
        top = jnp.maximum(jnp.max(jnp.abs(total), keepdims=True), 1e-30)
        coded = jnp.round(total * (CODE_TOP / top))
        coded_ref[:, here] = coded.astype(jnp.int32).astype(coded_ref.dtype)
        step_ref[place : place + 1, :] = jnp.broadcast_to(
            top * (1.0 / CODE_TOP), (1, step_ref.shape[1])
        )


def join_coded(partial, pooled, w):
    return pl.pallas_call(
        join_coded_kernel,
        out_shape=(
            jax.ShapeDtypeStruct(partial.shape, jnp.int16),
            jax.ShapeDtypeStruct((8, 128), jnp.float32),
        ),
        in_specs=[ON_CHIP] * 3,
        out_specs=(ON_CHIP,) * 2,
        name="join_coded",
        **options(),
    )(partial, pooled, w)


def second_kernel(w_ref, preact_ref, *refs):
    *received_refs, out_ref = refs
    outputs = None
    for place, here in enumerate(code_chunks(preact_ref.shape[1])):
        preact = preact_ref[:, here]
        for coded_ref, step_ref in zip(received_refs[::2], received_refs[1::2]):
            coded = coded_ref[:, here].astype(jnp.int32).astype(jnp.float32)
            preact = preact + coded * step_ref[place : place + 1, 0:1]
        hidden = jnp.maximum(preact, 0.0).astype(jnp.bfloat16)
        part = multiply(hidden, w_ref[here, :])
        outputs = part if outputs is None else outputs + part
    out_ref[...] = outputs.astype(out_ref.dtype)


def second_layer(w, preact, received):
    return pl.pallas_call(
        second_kernel,
        out_shape=jax.ShapeDtypeStruct((preact.shape[0], w.shape[1]), jnp.bfloat16),
        in_specs=[ON_CHIP] * (2 + len(received)),
        out_specs=ON_CHIP,
        name="second_layer",
        **options(),
    )(w, preact, *received)


def score_terms(blocks, pairs, head_ref, interact_ref, towers):
    width = head_ref.shape[0] // towers
    total = None
    for block, tower in blocks:
        rows_of_head = pl.ds(pl.multiple_of(tower * width, width), width)
        part = multiply(block, head_ref[rows_of_head, :])
        total = part if total is None else total + part
    for (one, t), (two, s) in pairs:
        gram = jnp.sum(one.astype(jnp.float32) * two.astype(jnp.float32), axis=1, keepdims=True)
        weights = interact_ref[pl.ds(t * towers + s, 1), :]
        if one is not two:
            weights = weights + interact_ref[pl.ds(s * towers + t, 1), :]
        total = total + gram * (weights * (1.0 / math.sqrt(width)))
    return total


def pairs_among(blocks):
    return [(blocks[i], blocks[j]) for i in range(len(blocks)) for j in range(i, len(blocks))]


def blocks_in(ref, masks):
    rows = ref.shape[0] // len(masks)
    me = lax.axis_index("tower")
    return [(ref[i * rows : (i + 1) * rows, :], me ^ mask) for i, mask in enumerate(masks)]


def score_kernel(masks, towers, *refs):
    *held_refs, head_ref, interact_ref, scores_ref = refs
    first = len(masks) == len(held_refs)
    if first:
        blocks = [b for ref, some in zip(held_refs, masks) for b in blocks_in(ref, some)]
        scores_ref[...] = score_terms(
            blocks, pairs_among(blocks), head_ref, interact_ref, towers
        )
    else:
        so_far_ref, *held_refs = held_refs
        kept = blocks_in(held_refs[0], masks[0])
        new = [b for ref, some in zip(held_refs[1:], masks[1:]) for b in blocks_in(ref, some)]
        pairs = [(one, two) for one in kept for two in new] + pairs_among(new)
        scores_ref[...] = so_far_ref[...] + score_terms(
            new, pairs, head_ref, interact_ref, towers
        )


def score(held, masks, head, interact, towers, so_far=None):
    operands = ([] if so_far is None else [so_far]) + list(held) + [head, interact]
    rows = held[0].shape[0] // len(masks[0])
    return pl.pallas_call(
        lambda *refs: score_kernel(masks, towers, *refs),
        out_shape=jax.ShapeDtypeStruct((rows, head.shape[1]), jnp.float32),
        in_specs=[ON_CHIP] * len(operands),
        out_specs=ON_CHIP,
        name="score",
        **options(),
    )(*operands)


def piece_kernel(low, ks, held_ref, after_hbm, *out_refs):
    group = held_ref.shape[1]
    place = lax.rem(lax.axis_index("tower") // low, group)
    for k, out_ref in zip(ks, out_refs):
        out_ref[...] = held_ref[:, place ^ k]


def pieces(held, low, ks, after):
    shape = jax.ShapeDtypeStruct((held.shape[0], *held.shape[2:]), held.dtype)
    return pl.pallas_call(
        lambda *refs: piece_kernel(low, ks, *refs),
        out_shape=(shape,) * len(ks),
        in_specs=[ON_CHIP, ANYWHERE],
        out_specs=(ON_CHIP,) * len(ks),
        name="pieces",
        **options(),
    )(held, after)


def exchange(blocks):
    towers, rows, width = blocks.shape
    assert towers & (towers - 1) == 0
    held, masks = blocks, (0,)
    low = 1
    while True:
        group = min(4, towers // low)
        split = held.reshape(held.shape[0] // group, group, *held.shape[1:])
        parts = [None] * group
        after = split
        for k in range(group - 1, 0, -1):
            if k > 1:
                (after,) = pieces(split, low, (k,), after)
                part = after
            else:
                part, parts[0] = pieces(split, low, (1, 0), after)
            parts[k] = lax.ppermute(part, "tower", [(i, i ^ (k * low)) for i in range(towers)])
        groups = tuple(tuple(k * low + mask for mask in masks) for k in range(group))
        if low * group == towers:
            return [part[0] for part in parts], groups
        joined = jnp.zeros_like(split)
        for k in range(group - 1, -1, -1):
            joined = lax.dynamic_update_index_in_dim(joined, parts[k], k, 1)
        held = joined.reshape(split.shape[0], group * held.shape[1], width)
        masks = sum(groups, ())
        low *= group


def on_device(ids, tables, order, w_first, w_second, w_head, w_interact):
    towers = lax.axis_size("tower")
    devices = lax.axis_size("dev")
    samples = ids.shape[2]
    my_rows = samples // devices
    order = order.reshape(devices, my_rows)
    ids, tables, w_first = jnp.swapaxes(ids[0], 1, 2), tables[0], w_first[0]

    def swap_cores(array):
        return lax.ppermute(array, "dev", [(i, i ^ 1) for i in range(devices)])

    w_other = swap_cores(w_first)
    away = tuple(range(1, devices // 2))
    pooled, order, ids, tables, w_first, residues, weights = first_pool(
        away, order, ids, tables, w_first
    )
    pooled = swap_cores(pooled)
    partial = away_layer(residues, weights, tables, w_first)
    partial, step = join_coded(partial, pooled, w_other)
    pooled, preact, partial, step = home_early(order, ids, tables, w_first, partial, step)
    received = []
    for place, chips_on in enumerate(away):
        onward = [(i, (i + 2 * chips_on) % devices) for i in range(devices)]
        block = partial[place * my_rows : (place + 1) * my_rows]
        received += [lax.ppermute(block, "dev", onward), lax.ppermute(step, "dev", onward)]
    pooled, preact = home_late(order, ids, tables, w_first, pooled, preact, partial)
    preact = join(preact, swap_cores(pooled), w_other)
    w_head, w_interact = fetch_head(w_head, w_interact, preact)
    outputs = second_layer(w_second[0], preact, received)
    held, masks = exchange(outputs.reshape(towers, my_rows // towers, outputs.shape[1]))
    so_far = score(held[:1], masks[:1], w_head, w_interact, towers)
    return score(held, masks, w_head, w_interact, towers, so_far)[None]


def solution(mesh):
    return jax.shard_map(
        on_device,
        mesh=mesh,
        in_specs=(
            P("tower", "dev", None, None),
            P("tower", "dev", None, None),
            P(),
            P("tower", "dev", None),
            P("tower", None, None),
            P(),
            P(),
        ),
        out_specs=P("dev", "tower", None),
        check_vma=False,
    )
```

```python
import math

import jax
import jax.numpy as jnp
from jax import lax
from jax.experimental import pallas as pl
from jax.experimental.pallas import tpu as pltpu
from jax.sharding import PartitionSpec as P

WORD_BITS = 32
CODE_TOP = 32767.0


def multiply(left, right):
    return jnp.dot(left, right, preferred_element_type=jnp.float32)


def one_hot(order_row, samples):
    rows = order_row.shape[1]
    pick = lax.broadcasted_iota(jnp.int32, (samples, rows), 0) == order_row
    return jnp.where(pick, 1.0, 0.0).astype(jnp.bfloat16)


def select_ids(ids, picks, residues):
    feats, bag, samples = ids.shape
    shift = residues.bit_length() - 1
    flat = ids.reshape(feats * bag, samples)
    low = (flat & (residues - 1)).astype(jnp.float32).astype(jnp.bfloat16)
    high = (flat >> shift).astype(jnp.float32).astype(jnp.bfloat16)
    both = multiply(jnp.concatenate([low, high], axis=0), picks).astype(jnp.int32)
    return both[: feats * bag, :], jnp.left_shift(1, both[feats * bag :, :])


def bit_planes(hits):
    waiting = []

    def push(level, bits):
        if level == len(waiting):
            waiting.append([])
        queue = waiting[level]
        queue.append(bits)
        if len(queue) == 3:
            first, second, third = queue
            both = first ^ second
            waiting[level] = [both ^ third]
            push(level + 1, (first & second) | (both & third))

    for bits in hits:
        push(0, bits)
    level = 0
    while level < len(waiting):
        if len(waiting[level]) == 2:
            first, second = waiting[level]
            waiting[level] = [first ^ second]
            push(level + 1, first & second)
        level += 1
    return [queue[0] for queue in waiting]


def merge(low, high, width, mask, second):
    shift = width if second else 0
    low = (low >> shift) & mask if low is not None else None
    if high is None:
        return low
    high = ((high >> shift) & mask) << width
    return high if low is None else low | high


def byte_fields(planes):
    planes = planes + [None] * (8 - len(planes))
    pairs = [
        [merge(planes[p], planes[p + 1], 1, 0x55555555, odd) for odd in (0, 1)]
        for p in range(0, 8, 2)
    ]
    fours = [
        [[merge(pairs[p][a], pairs[p + 1][a], 2, 0x33333333, odd) for odd in (0, 1)] for a in (0, 1)]
        for p in (0, 2)
    ]
    return [
        merge(fours[0][i & 1][(i >> 1) & 1], fours[1][i & 1][(i >> 1) & 1], 4, 0x0F0F0F0F, i >> 2)
        for i in range(8)
    ]


def count_ids(residue_ref, weight_ref, base, bag, active):
    residues = active // WORD_BITS
    spots = lax.broadcasted_iota(jnp.int32, (residues, residue_ref.shape[1]), 0)
    hits = (
        jnp.where(residue_ref[pl.ds(at, 1), :] == spots, weight_ref[pl.ds(at, 1), :], 0)
        for at in range(base, base + bag)
    )
    words = jnp.concatenate(byte_fields(bit_planes(hits)), axis=0).T
    return jnp.concatenate(
        [
            ((words >> (8 * place)) & 255).astype(jnp.float32).astype(jnp.bfloat16)
            for place in range(4)
        ],
        axis=1,
    )


def pool_feature(residue_ref, weight_ref, base, bag, table):
    counts = count_ids(residue_ref, weight_ref, base, bag, table.shape[0])
    return multiply(counts, table).astype(jnp.bfloat16)


def pick_rows(targets, order_ref, samples):
    picks = [one_hot(order_ref[pl.ds(target, 1), :], samples) for target in targets]
    return jnp.concatenate(picks, axis=1)


def pick_ids(targets, ids, order_ref, active):
    return select_ids(ids, pick_rows(targets, order_ref, ids.shape[2]), active // WORD_BITS)


def block_of(chips_on, core_flip, devices):
    return lax.rem((lax.axis_index("dev") ^ core_flip) + 2 * chips_on, devices)


def start_copies(source, target, sem, parts):
    size = source.shape[0] // parts
    for part in range(parts):
        here = pl.ds(part * size, size)
        pltpu.make_async_copy(source.at[here], target.at[here], sem).start()
    return pltpu.make_async_copy(source, target, sem)


def first_kernel(
    blocks, order_hbm, ids_hbm, tables_hbm, w_hbm,
    out_ref, order_ref, ids_ref, tables_ref, w_ref, residues_ref, weights_ref,
    residue_ref, weight_ref, picks_ref, sems,
):
    devices, rows = order_hbm.shape
    feats, bag, samples = ids_hbm.shape
    active, emb = tables_hbm.shape[1:]
    order_here = start_copies(order_hbm, order_ref, sems.at[0], 1)
    ids_here = start_copies(ids_hbm, ids_ref, sems.at[1], 1)
    tables_here = start_copies(tables_hbm, tables_ref, sems.at[2], 1)
    w_here = start_copies(w_hbm, w_ref, sems.at[3], 2)
    order_here.wait()
    for block, chips_on in enumerate(blocks):
        picks = pick_rows(
            (block_of(chips_on, 1, devices), block_of(chips_on, 0, devices)), order_ref, samples
        )
        if block == 0:
            picks_ref[...] = picks
            ids_here.wait()
            picks = picks_ref[...]
        residue, weight = select_ids(ids_ref[...], picks, active // WORD_BITS)
        residue_ref[...], weight_ref[...] = residue[:, :rows], weight[:, :rows]
        residues_ref[block], weights_ref[block] = residue[:, rows:], weight[:, rows:]
        if block == 0:
            tables_here.wait()
        for feature in range(feats):
            out_ref[block * rows : (block + 1) * rows, feature * emb : (feature + 1) * emb] = (
                pool_feature(residue_ref, weight_ref, feature * bag, bag, tables_ref[feature])
            )
    w_here.wait()


def layer_block(residue_ref, weight_ref, bag, tables_ref, w_ref):
    feats, active, emb = tables_ref.shape
    total = None
    for first in range(0, feats, 2):
        some = range(first, min(first + 2, feats))
        pooled = [
            pool_feature(residue_ref, weight_ref, feature * bag, bag, tables_ref[feature])
            for feature in some
        ]
        part = multiply(
            jnp.concatenate(pooled, axis=1), w_ref[first * emb : (first + len(some)) * emb, :]
        )
        total = part if total is None else total + part
    return total


def away_kernel(residues_ref, weights_ref, tables_ref, w_ref, out_ref):
    count, picked, rows = residues_ref.shape
    bag = picked // tables_ref.shape[0]
    for block in range(count):
        out_ref[block * rows : (block + 1) * rows, :] = layer_block(
            residues_ref.at[block], weights_ref.at[block], bag, tables_ref, w_ref
        )


def home_rows(order_ref, ids_ref, tables_ref, w_ref, pooled_ref, out_ref, residue_ref, weight_ref):
    devices, rows = order_ref.shape
    feats, bag, samples = ids_ref.shape
    active, emb = tables_ref.shape[1:]
    residue, weight = pick_ids(
        (block_of(0, 1, devices), block_of(0, 0, devices)), ids_ref[...], order_ref, active
    )
    residue_ref[...], weight_ref[...] = residue, weight
    other, mine = slice(0, rows), slice(rows, 2 * rows)
    for feature in range(feats):
        pooled_ref[:, feature * emb : (feature + 1) * emb] = pool_feature(
            residue_ref.at[:, other], weight_ref.at[:, other], feature * bag, bag, tables_ref[feature]
        )
    out_ref[...] = layer_block(
        residue_ref.at[:, mine], weight_ref.at[:, mine], bag, tables_ref, w_ref
    )


def early_kernel(
    order_ref, ids_ref, tables_ref, w_ref, partial_ref, step_ref,
    pooled_ref, out_ref, again_ref, step_again_ref, residue_ref, weight_ref,
):
    @pl.when(lax.axis_index("dev") % 2 == 1)
    def _():
        home_rows(
            order_ref, ids_ref, tables_ref, w_ref, pooled_ref, out_ref, residue_ref, weight_ref
        )

    again_ref[...] = partial_ref[...]
    step_again_ref[...] = step_ref[...]


def late_kernel(
    order_ref, ids_ref, tables_ref, w_ref, pooled_in_ref, in_ref, after_hbm,
    pooled_ref, out_ref, residue_ref, weight_ref,
):
    second = lax.axis_index("dev") % 2 == 1

    @pl.when(second)
    def _():
        pooled_ref[...] = pooled_in_ref[...]
        out_ref[...] = in_ref[...]

    @pl.when(jnp.logical_not(second))
    def _():
        home_rows(
            order_ref, ids_ref, tables_ref, w_ref, pooled_ref, out_ref, residue_ref, weight_ref
        )


IN_HBM = pl.BlockSpec(memory_space=pltpu.HBM)
ON_CHIP = pl.BlockSpec(memory_space=pltpu.VMEM)
ANYWHERE = pl.BlockSpec(memory_space=pl.ANY)
VMEM_LIMIT = 16 * 1024 * 1024


def in_hbm(*arrays):
    return [pltpu.with_memory_space_constraint(array, pltpu.HBM) for array in arrays]


def like(array):
    return jax.ShapeDtypeStruct(array.shape, array.dtype)


def picked(ids, rows):
    return [pltpu.VMEM((ids.shape[0] * ids.shape[1], rows), jnp.int32)] * 2


def options():
    return {
        "compiler_params": pltpu.CompilerParams(vmem_limit_bytes=VMEM_LIMIT),
        "cost_estimate": pl.CostEstimate(flops=1, bytes_accessed=1, transcendentals=0),
    }


def first_pool(blocks, order, ids, tables, w):
    rows = order.shape[1]
    feats, bag = ids.shape[:2]
    chosen = jax.ShapeDtypeStruct((len(blocks), feats * bag, rows), jnp.int32)
    return pl.pallas_call(
        lambda *refs: first_kernel(blocks, *refs),
        out_shape=(
            jax.ShapeDtypeStruct((len(blocks) * rows, feats * tables.shape[2]), jnp.bfloat16),
            like(order), like(ids), like(tables), like(w), chosen, chosen,
        ),
        in_specs=[IN_HBM] * 4,
        out_specs=(ON_CHIP,) * 7,
        scratch_shapes=picked(ids, rows)
        + [pltpu.VMEM((ids.shape[2], 2 * rows), jnp.bfloat16), pltpu.SemaphoreType.DMA((4,))],
        name="first_pool",
        **options(),
    )(*in_hbm(order, ids, tables, w))


def away_layer(residues, weights, tables, w):
    return pl.pallas_call(
        away_kernel,
        out_shape=jax.ShapeDtypeStruct((residues.shape[0] * residues.shape[2], w.shape[1]), jnp.float32),
        in_specs=[ON_CHIP] * 4,
        out_specs=ON_CHIP,
        name="away_layer",
        **options(),
    )(residues, weights, tables, w)


def home_shapes(order, ids, tables, w):
    rows = order.shape[1]
    return (
        jax.ShapeDtypeStruct((rows, ids.shape[0] * tables.shape[2]), jnp.bfloat16),
        jax.ShapeDtypeStruct((rows, w.shape[1]), jnp.float32),
    )


def home_early(order, ids, tables, w, partial, step):
    return pl.pallas_call(
        early_kernel,
        out_shape=home_shapes(order, ids, tables, w) + (like(partial), like(step)),
        in_specs=[ON_CHIP] * 6,
        out_specs=(ON_CHIP,) * 4,
        scratch_shapes=picked(ids, 2 * order.shape[1]),
        name="home_early",
        **options(),
    )(order, ids, tables, w, partial, step)


def home_late(order, ids, tables, w, pooled, preact, after):
    return pl.pallas_call(
        late_kernel,
        out_shape=home_shapes(order, ids, tables, w),
        in_specs=[ON_CHIP] * 6 + [ANYWHERE],
        out_specs=(ON_CHIP,) * 2,
        scratch_shapes=picked(ids, 2 * order.shape[1]),
        name="home_late",
        **options(),
    )(order, ids, tables, w, pooled, preact, after)


def fetch_kernel(head_hbm, interact_hbm, after_hbm, head_ref, interact_ref, sems):
    copies = (
        start_copies(head_hbm, head_ref, sems.at[0], 8),
        start_copies(interact_hbm, interact_ref, sems.at[1], 1),
    )
    for copy in copies:
        copy.wait()


def fetch_head(head, interact, after):
    return pl.pallas_call(
        fetch_kernel,
        out_shape=(like(head), like(interact)),
        in_specs=[IN_HBM] * 2 + [ANYWHERE],
        out_specs=(ON_CHIP,) * 2,
        scratch_shapes=[pltpu.SemaphoreType.DMA((2,))],
        name="fetch_head",
        **options(),
    )(*in_hbm(head, interact), after)


def join_kernel(partial_ref, pooled_ref, w_ref, out_ref):
    out_ref[...] = partial_ref[...] + multiply(pooled_ref[...], w_ref[...])


def join(partial, pooled, w):
    return pl.pallas_call(
        join_kernel,
        out_shape=like(partial),
        in_specs=[ON_CHIP] * 3,
        out_specs=ON_CHIP,
        name="join",
        **options(),
    )(partial, pooled, w)


def code_chunks(width):
    count = max(1, min(8, width // 256))
    return [slice(i * width // count, (i + 1) * width // count) for i in range(count)]


def join_coded_kernel(partial_ref, pooled_ref, w_ref, coded_ref, step_ref):
    step_ref[...] = jnp.zeros_like(step_ref)
    for place, here in enumerate(code_chunks(partial_ref.shape[1])):
        total = partial_ref[:, here] + multiply(pooled_ref[...], w_ref[:, here])
        top = jnp.maximum(jnp.max(jnp.abs(total), keepdims=True), 1e-30)
        coded = jnp.round(total * (CODE_TOP / top))
        coded_ref[:, here] = coded.astype(jnp.int32).astype(coded_ref.dtype)
        step_ref[place : place + 1, :] = jnp.broadcast_to(
            top * (1.0 / CODE_TOP), (1, step_ref.shape[1])
        )


def join_coded(partial, pooled, w):
    return pl.pallas_call(
        join_coded_kernel,
        out_shape=(
            jax.ShapeDtypeStruct(partial.shape, jnp.int16),
            jax.ShapeDtypeStruct((8, 128), jnp.float32),
        ),
        in_specs=[ON_CHIP] * 3,
        out_specs=(ON_CHIP,) * 2,
        name="join_coded",
        **options(),
    )(partial, pooled, w)


def second_kernel(w_ref, preact_ref, *refs):
    *received_refs, out_ref = refs
    outputs = None
    for place, here in enumerate(code_chunks(preact_ref.shape[1])):
        preact = preact_ref[:, here]
        for coded_ref, step_ref in zip(received_refs[::2], received_refs[1::2]):
            coded = coded_ref[:, here].astype(jnp.int32).astype(jnp.float32)
            preact = preact + coded * step_ref[place : place + 1, 0:1]
        hidden = jnp.maximum(preact, 0.0).astype(jnp.bfloat16)
        part = multiply(hidden, w_ref[here, :])
        outputs = part if outputs is None else outputs + part
    out_ref[...] = outputs.astype(out_ref.dtype)


def second_layer(w, preact, received):
    return pl.pallas_call(
        second_kernel,
        out_shape=jax.ShapeDtypeStruct((preact.shape[0], w.shape[1]), jnp.bfloat16),
        in_specs=[ON_CHIP] * (2 + len(received)),
        out_specs=ON_CHIP,
        name="second_layer",
        **options(),
    )(w, preact, *received)


def score_terms(blocks, pairs, head_ref, interact_ref, towers):
    width = head_ref.shape[0] // towers
    total = None
    for block, tower in blocks:
        rows_of_head = pl.ds(pl.multiple_of(tower * width, width), width)
        part = multiply(block, head_ref[rows_of_head, :])
        total = part if total is None else total + part
    for (one, t), (two, s) in pairs:
        gram = jnp.sum(one.astype(jnp.float32) * two.astype(jnp.float32), axis=1, keepdims=True)
        weights = interact_ref[pl.ds(t * towers + s, 1), :]
        if one is not two:
            weights = weights + interact_ref[pl.ds(s * towers + t, 1), :]
        total = total + gram * (weights * (1.0 / math.sqrt(width)))
    return total


def pairs_among(blocks):
    return [(blocks[i], blocks[j]) for i in range(len(blocks)) for j in range(i, len(blocks))]


def blocks_in(ref, masks):
    rows = ref.shape[0] // len(masks)
    me = lax.axis_index("tower")
    return [(ref[i * rows : (i + 1) * rows, :], me ^ mask) for i, mask in enumerate(masks)]


def score_kernel(masks, towers, *refs):
    *held_refs, head_ref, interact_ref, scores_ref = refs
    first = len(masks) == len(held_refs)
    if first:
        blocks = [b for ref, some in zip(held_refs, masks) for b in blocks_in(ref, some)]
        scores_ref[...] = score_terms(
            blocks, pairs_among(blocks), head_ref, interact_ref, towers
        )
    else:
        so_far_ref, *held_refs = held_refs
        kept = blocks_in(held_refs[0], masks[0])
        new = [b for ref, some in zip(held_refs[1:], masks[1:]) for b in blocks_in(ref, some)]
        pairs = [(one, two) for one in kept for two in new] + pairs_among(new)
        scores_ref[...] = so_far_ref[...] + score_terms(
            new, pairs, head_ref, interact_ref, towers
        )


def score(held, masks, head, interact, towers, so_far=None):
    operands = ([] if so_far is None else [so_far]) + list(held) + [head, interact]
    rows = held[0].shape[0] // len(masks[0])
    return pl.pallas_call(
        lambda *refs: score_kernel(masks, towers, *refs),
        out_shape=jax.ShapeDtypeStruct((rows, head.shape[1]), jnp.float32),
        in_specs=[ON_CHIP] * len(operands),
        out_specs=ON_CHIP,
        name="score",
        **options(),
    )(*operands)


def piece_kernel(low, ks, held_ref, after_hbm, *out_refs):
    group = held_ref.shape[1]
    place = lax.rem(lax.axis_index("tower") // low, group)
    for k, out_ref in zip(ks, out_refs):
        out_ref[...] = held_ref[:, place ^ k]


def pieces(held, low, ks, after):
    shape = jax.ShapeDtypeStruct((held.shape[0], *held.shape[2:]), held.dtype)
    return pl.pallas_call(
        lambda *refs: piece_kernel(low, ks, *refs),
        out_shape=(shape,) * len(ks),
        in_specs=[ON_CHIP, ANYWHERE],
        out_specs=(ON_CHIP,) * len(ks),
        name="pieces",
        **options(),
    )(held, after)


def exchange(blocks, after):
    towers, rows, width = blocks.shape
    assert towers & (towers - 1) == 0
    held, masks = blocks, (0,)
    low = 1
    while True:
        group = min(4, towers // low)
        split = held.reshape(held.shape[0] // group, group, *held.shape[1:])
        parts = [None] * group
        for k in range(group - 1, 0, -1):
            if k > 1:
                (after,) = pieces(split, low, (k,), after)
                part = after
            else:
                part, parts[0] = pieces(split, low, (1, 0), after)
            parts[k] = lax.ppermute(part, "tower", [(i, i ^ (k * low)) for i in range(towers)])
        groups = tuple(tuple(k * low + mask for mask in masks) for k in range(group))
        if low * group == towers:
            return [part[0] for part in parts], groups
        joined = jnp.zeros_like(split)
        for k in range(group - 1, -1, -1):
            joined = lax.dynamic_update_index_in_dim(joined, parts[k], k, 1)
        held = joined.reshape(split.shape[0], group * held.shape[1], width)
        masks = sum(groups, ())
        low *= group


def on_device(ids, tables, order, w_first, w_second, w_head, w_interact):
    towers = lax.axis_size("tower")
    devices = lax.axis_size("dev")
    samples = ids.shape[2]
    my_rows = samples // devices
    order = order.reshape(devices, my_rows)
    ids, tables, w_first = jnp.swapaxes(ids[0], 1, 2), tables[0], w_first[0]

    def swap_cores(array):
        return lax.ppermute(array, "dev", [(i, i ^ 1) for i in range(devices)])

    w_other = swap_cores(w_first)
    away = tuple(range(1, devices // 2))
    pooled, order, ids, tables, w_first, residues, weights = first_pool(
        away, order, ids, tables, w_first
    )
    pooled = swap_cores(pooled)
    partial = away_layer(residues, weights, tables, w_first)
    partial, step = join_coded(partial, pooled, w_other)
    pooled, preact, partial, step = home_early(order, ids, tables, w_first, partial, step)
    received = []
    for place, chips_on in enumerate(away):
        onward = [(i, (i + 2 * chips_on) % devices) for i in range(devices)]
        block = partial[place * my_rows : (place + 1) * my_rows]
        received += [lax.ppermute(block, "dev", onward), lax.ppermute(step, "dev", onward)]
    pooled, preact = home_late(order, ids, tables, w_first, pooled, preact, partial)
    preact = join(preact, swap_cores(pooled), w_other)
    w_head, w_interact = fetch_head(w_head, w_interact, preact)
    outputs = second_layer(w_second[0], preact, received)
    held, masks = exchange(outputs.reshape(towers, my_rows // towers, outputs.shape[1]), w_head)
    so_far = score(held[:1], masks[:1], w_head, w_interact, towers)
    return score(held, masks, w_head, w_interact, towers, so_far)[None]


def solution(mesh):
    return jax.shard_map(
        on_device,
        mesh=mesh,
        in_specs=(
            P("tower", "dev", None, None),
            P("tower", "dev", None, None),
            P(),
            P("tower", "dev", None),
            P("tower", None, None),
            P(),
            P(),
        ),
        out_specs=P("dev", "tower", None),
        check_vma=False,
    )
```
